256 devices in a mesh: group: 16 (over y_lo, x, core), tensor: 16 (over y_hi, z).
Axes of the slice: x: 4, y: 4 (y_hi: 2, y_lo: 2; y = y_hi * 2 + y_lo), z: 8, core: 2. Of those that a mesh axis runs over, the one named last changes fastest.
Arguments:
- queries: bfloat16 [4, 256, 64, 128], P(None, 'group', 'tensor')
- new_keys: bfloat16 [4, 256, 16, 128], P(None, 'group', 'tensor')
- new_values: bfloat16 [4, 256, 16, 128], P(None, 'group', 'tensor')
- key_cache: bfloat16 [256, 16, 512, 128], P('group', 'tensor')
- value_cache: bfloat16 [256, 16, 512, 128], P('group', 'tensor')
- cache_len: int32 [256], replicated, may hold values from 8 to 508, as said below
- remaining: int32 [256], replicated, may hold values from 0 to 6
- dest_table: int32 [256], replicated, may hold values from 0 to 255, as said below
- residual_in: bfloat16 [4, 256, 5120], P(None, 'group')
- out_weight: bfloat16 [8192, 5120], P('tensor'), may hold values from -0.0625 to 0.0625
- norm_gain: bfloat16 [5120], replicated, may hold values from 0.5 to 1.5
Outputs:
- residual_out: bfloat16 [4, 256, 5120], P(None, 'group')
- normed: bfloat16 [4, 256, 5120], P(None, 'group')
- key_out: bfloat16 [256, 16, 512, 128], P('group', 'tensor')
- value_out: bfloat16 [256, 16, 512, 128], P('group', 'tensor')
The draws below stay inside these ranges and needn't reach their ends.
Inputs may be any that keep to these rules, and one draw needn't show every extreme that they name: dest_table is a permutation of the 256 slots, old slot g * 16 + j being slot j of group g. Each group sends exactly one of its sequences to every group, itself included, and the one that group g sends lands in slot g of its new group (dest_table % 16 equals the sending group). `cache_len`: some sequence has exactly 508 cached tokens in every draw.
All inputs are finite; a program needn't handle non-finite values.
Results may differ from the reference program's by a relative error of at most 0.0033.
Values may be sent and summed in bfloat16 or wider, within the bound.
No kernel may reach another device: no remote copies, remote signals or barrier semaphores. Data moves between devices by JAX's collectives and lax.ppermute only.
A program may use at most 128 MiB of HBM per device.

```python
import jax
import jax.numpy as jnp
from jax import lax

D = 5120
HEADS = 64
KV_HEADS = 8
HEAD_DIM = 128
STEPS = 4
LMAX = 512
SLOTS = 16
SEQS = 256
KV_COPIES = 16


def repeat_copies(array, axis):
    return jnp.repeat(array, KV_COPIES // KV_HEADS, axis=axis)


def draw_queries(key, part):
    key = jax.random.fold_in(key, 1)
    shape = (STEPS, SEQS, HEADS, HEAD_DIM)
    result = jnp.clip(jax.random.normal(key, shape, jnp.float32), -6.0, 6.0)
    return result.astype(jnp.bfloat16)


def draw_new_keys(key, part):
    key = jax.random.fold_in(key, 2)
    shape = (STEPS, SEQS, KV_HEADS, HEAD_DIM)
    result = repeat_copies(jnp.clip(jax.random.normal(key, shape, jnp.float32), -6.0, 6.0), 2)
    return result.astype(jnp.bfloat16)


def draw_new_values(key, part):
    key = jax.random.fold_in(key, 7)
    shape = (STEPS, SEQS, KV_HEADS, HEAD_DIM)
    result = jnp.clip(3.0 * jax.random.normal(key, shape, jnp.float32), -12.0, 12.0)
    return repeat_copies(result, 2).astype(jnp.bfloat16)


def draw_key_cache(key, part):
    key = jax.random.fold_in(key, 3)
    shape = (SEQS, KV_HEADS, LMAX, HEAD_DIM)
    result = repeat_copies(jnp.clip(jax.random.normal(key, shape, jnp.float32), -6.0, 6.0), 1)
    return result.astype(jnp.bfloat16)


def draw_value_cache(key, part):
    key = jax.random.fold_in(key, 8)
    shape = (SEQS, KV_HEADS, LMAX, HEAD_DIM)
    result = jnp.clip(3.0 * jax.random.normal(key, shape, jnp.float32), -12.0, 12.0)
    return repeat_copies(result, 1).astype(jnp.bfloat16)


def draw_residual_in(key, part):
    key = jax.random.fold_in(key, 4)
    noise_key, row_key = jax.random.split(key)
    shape = (STEPS, SEQS, D)
    column = jnp.arange(D, dtype=jnp.float32) / D
    noise = jnp.clip(jax.random.normal(noise_key, shape, jnp.float32), -6.0, 6.0)
    column_scale = 10.0 ** column
    row_scale = 10.0 ** jax.random.uniform(row_key, (STEPS, SEQS, 1), jnp.float32, 0.0, 1.0)
    return (0.05 * noise * row_scale * column_scale).astype(jnp.bfloat16)


def draw_cache_len(key, part):
    key = jax.random.fold_in(key, 5)
    base_key, high_key, pick_key, spot_key = jax.random.split(key, 4)
    top_len = LMAX - STEPS
    base = jax.random.randint(base_key, (SEQS,), 8, top_len + 1)
    high = jax.random.randint(high_key, (SEQS,), LMAX // 2, top_len + 1)
    picked = jax.random.randint(pick_key, (SEQS,), 0, 10) < 3
    lengths = jnp.where(picked, high, base)
    chosen_spot = jax.random.randint(spot_key, (), 0, SEQS)
    return jnp.where(jnp.arange(SEQS, dtype=jnp.int32) == chosen_spot, top_len, lengths).astype(jnp.int32)


def one_permutation(single_key):
    return jax.random.permutation(single_key, SLOTS)


def draw_dest_table(key, part):
    key = jax.random.fold_in(key, 6)
    group_count = SEQS // SLOTS
    group_keys = jax.random.split(key, group_count)
    offsets = jax.vmap(one_permutation)(group_keys).astype(jnp.int32)
    anchor = jnp.arange(group_count, dtype=jnp.int32)[:, None]
    table = (anchor + offsets) % group_count * SLOTS + anchor
    return table.reshape(SEQS).astype(jnp.int32)


def place_ends(entries, key, low, high):
    extent = entries.shape
    place = [jax.random.randint(jax.random.fold_in(key, axis), (), 0, extent[axis]) for axis in range(len(extent))]
    entries = entries.at[tuple(place)].set(low)
    longest = extent.index(max(extent))
    place[longest] = (place[longest] + 1) % extent[longest]
    return entries.at[tuple(place)].set(high)


def block_scale(stream_key, shape, cuts, least, top_value):
    gain = 1.0
    for dim, blocks in cuts:
        steps = jax.random.uniform(jax.random.fold_in(jax.random.fold_in(stream_key, 6), dim), (blocks,), jnp.float32, least / len(cuts), top_value / len(cuts))
        gain = gain * jnp.repeat(jnp.exp(steps), shape[dim] // blocks).reshape((-1,) + (1,) * (len(shape) - 1 - dim))
    return gain


def scatter_about(key, shape, scale, bound, shards=(), kind=jnp.bfloat16):
    values = jax.random.normal(key, shape, jnp.float32) * scale
    if len(shards) > 0:
        values = block_scale(key, shape, shards, -0.22, 0.18) * values
    return jnp.clip(values, min=-bound, max=bound).astype(kind)


def setup_inputs(seed: int = 0) -> dict:
    key_list = jax.random.split(jax.random.key(seed), 12)
    queries = draw_queries(jax.random.fold_in(key_list[11], 71), 0)
    new_keys = draw_new_keys(jax.random.fold_in(key_list[11], 71), 0)
    new_values = draw_new_values(jax.random.fold_in(key_list[11], 71), 0)
    key_cache = draw_key_cache(jax.random.fold_in(key_list[11], 71), 0)
    value_cache = draw_value_cache(jax.random.fold_in(key_list[11], 71), 0)
    cache_len = draw_cache_len(jax.random.fold_in(key_list[11], 71), 0)
    remaining = place_ends(jax.random.randint(key_list[6], (SEQS,), 0, 7), jax.random.fold_in(key_list[6], 1), 0, 6).astype(jnp.int32)
    dest_table = draw_dest_table(jax.random.fold_in(key_list[11], 71), 0)
    residual_in = draw_residual_in(jax.random.fold_in(key_list[11], 71), 0)
    out_weight = scatter_about(key_list[9], (HEADS * HEAD_DIM, D), (HEADS * HEAD_DIM) ** -0.5, 0.0625, ((0, 16),))
    norm_gain = jnp.clip(1.0 + 0.1 * jax.random.normal(key_list[10], (D,), jnp.float32), 0.5, 1.5).astype(jnp.bfloat16)
    return dict(queries=queries, new_keys=new_keys, new_values=new_values, key_cache=key_cache, value_cache=value_cache, cache_len=cache_len, remaining=remaining, dest_table=dest_table, residual_in=residual_in, out_weight=out_weight, norm_gain=norm_gain)


neg_fill = -1e+30
eps = 1e-06

def weigh(scores):
    top = lax.optimization_barrier(jnp.max(scores, axis=-1))
    weights = jnp.exp(scores - top[..., None])
    summed = lax.optimization_barrier(jnp.sum(weights, axis=-1))
    rounded = lax.optimization_barrier(weights.astype(jnp.bfloat16))
    return (top, rounded.astype(jnp.float32), summed)

def one_sequence(items):
    query_rows, fresh_keys, fresh_values, old_keys, old_values, length, rest = items
    group_size = HEADS // KV_COPIES
    scale = HEAD_DIM ** (-0.5)
    grouped = query_rows.astype(jnp.float32).reshape(STEPS, KV_COPIES, group_size, HEAD_DIM)
    places = jnp.arange(LMAX, dtype=jnp.int32)
    cache_scores = jnp.einsum('tkgd,kld->tkgl', grouped, old_keys.astype(jnp.float32), precision=lax.Precision.HIGHEST) * scale
    cache_scores = jnp.where(places < length, cache_scores, neg_fill)
    top_one, weight_one, total_one = weigh(cache_scores)
    mixed_one = jnp.einsum('tkgl,kld->tkgd', weight_one, old_values.astype(jnp.float32), precision=lax.Precision.HIGHEST)
    fresh_scores = jnp.einsum('tkgd,ukd->tkgu', grouped, fresh_keys.astype(jnp.float32), precision=lax.Precision.HIGHEST) * scale
    earlier = jnp.arange(STEPS, dtype=jnp.int32)[None, :] <= jnp.arange(STEPS, dtype=jnp.int32)[:, None]
    fresh_scores = jnp.where(earlier[:, None, None, :], fresh_scores, neg_fill)
    top_two, weight_two, total_two = weigh(fresh_scores)
    mixed_two = jnp.einsum('tkgu,ukd->tkgd', weight_two, fresh_values.astype(jnp.float32), precision=lax.Precision.HIGHEST)
    highest = jnp.maximum(top_one, top_two)
    first_factor = jnp.exp(top_one - highest)
    second_factor = jnp.exp(top_two - highest)
    merged = (first_factor[..., None] * mixed_one + second_factor[..., None] * mixed_two) / (first_factor * total_one + second_factor * total_two)[..., None]
    living = jnp.arange(STEPS, dtype=jnp.int32) < rest
    merged = jnp.where(living[:, None, None, None], merged, 0.0).astype(jnp.bfloat16).reshape(STEPS, HEADS * HEAD_DIM)
    retained = (places < length) & (rest > 0)
    key_new = jnp.where(retained[None, :, None], old_keys, jnp.zeros((), old_keys.dtype))
    value_new = jnp.where(retained[None, :, None], old_values, jnp.zeros((), old_values.dtype))
    for step in range(STEPS):
        placed = (places == length + step) & (step < rest)
        key_new = jnp.where(placed[None, :, None], fresh_keys[step][:, None, :], key_new)
        value_new = jnp.where(placed[None, :, None], fresh_values[step][:, None, :], value_new)
    return (merged, key_new, value_new)

def reference(queries, new_keys, new_values, key_cache, value_cache, cache_len, remaining, dest_table, residual_in, out_weight, norm_gain):
    source = jnp.zeros((SEQS,), jnp.int32).at[dest_table].set(jnp.arange(SEQS, dtype=jnp.int32))
    lengths = cache_len[source]
    rests = remaining[source]
    merged, key_out, value_out = lax.map(one_sequence, (jnp.swapaxes(queries, 0, 1), jnp.swapaxes(new_keys, 0, 1), jnp.swapaxes(new_values, 0, 1), key_cache[source], value_cache[source], lengths, rests))
    merged = jnp.swapaxes(merged, 0, 1).reshape(STEPS * SEQS, HEADS * HEAD_DIM)
    head_sum = jnp.dot(merged, out_weight, preferred_element_type=jnp.float32).reshape(STEPS, SEQS, D)
    level = residual_in.astype(jnp.float32) + head_sum
    scaled = level * lax.rsqrt(lax.optimization_barrier(jnp.mean(level * level, axis=-1, keepdims=True)) + eps) * norm_gain.astype(jnp.float32)
    return (level.astype(jnp.bfloat16), scaled.astype(jnp.bfloat16), key_out, value_out)
```

```python
import functools

import jax
import jax.numpy as jnp
from jax import lax
from jax.experimental import pallas as pl
from jax.experimental.pallas import tpu as pltpu
from jax.sharding import PartitionSpec as P

neg_fill = -1e30
eps = 1e-06
ORDER = (0, 8, 4, 12, 2, 10, 6, 14, 1, 9, 5, 13, 3, 11, 7, 15)
f32 = jnp.float32
bf16 = jnp.bfloat16


def order_kernel(table, keys, values, keys_out, values_out, sems):
    n = keys.shape[0]

    def copies(d):
        j = table[0, d]
        return (
            pltpu.make_async_copy(keys.at[j], keys_out.at[d], sems.at[0, d]),
            pltpu.make_async_copy(values.at[j], values_out.at[d], sems.at[1, d]),
        )

    for d in range(n):
        for c in copies(d):
            c.start()
    for d in range(n):
        for c in copies(d):
            c.wait()


def order_cache(table, keys, values):
    n = keys.shape[0]
    return pl.pallas_call(
        order_kernel,
        out_shape=(
            jax.ShapeDtypeStruct(keys.shape, keys.dtype),
            jax.ShapeDtypeStruct(values.shape, values.dtype),
        ),
        in_specs=[
            pl.BlockSpec(memory_space=pltpu.SMEM),
            pl.BlockSpec(memory_space=pl.ANY),
            pl.BlockSpec(memory_space=pl.ANY),
        ],
        out_specs=(pl.BlockSpec(memory_space=pl.ANY),) * 2,
        scratch_shapes=[pltpu.SemaphoreType.DMA((2, n))],
        cost_estimate=pl.CostEstimate(
            flops=0, bytes_accessed=4 * keys.size * 2, transcendentals=0
        ),
        name="order_cache",
    )(table, keys, values)


def attend_kernel(table, msg, keys, values, weight, keep, send, att, kbuf, vbuf, wbuf, sems):
    t = table[5, 0]
    n = msg.shape[0]
    slots = kbuf.shape[0]
    wcopy = pltpu.make_async_copy(weight, wbuf, sems.at[2, 0])

    def fetch(p):
        c = t ^ ORDER[p]
        s = p % slots
        return (
            pltpu.make_async_copy(keys.at[c], kbuf.at[s], sems.at[0, s]),
            pltpu.make_async_copy(values.at[c], vbuf.at[s], sems.at[1, s]),
        )

    for p in range(min(slots, n)):
        for c in fetch(p):
            c.start()
    wcopy.start()
    col = lax.broadcasted_iota(jnp.int32, (16, keys.shape[1]), 1)
    row8 = lax.broadcasted_iota(jnp.int32, (16, 8), 0) % 4
    col8 = lax.broadcasted_iota(jnp.int32, (16, 8), 1)
    rowd = lax.broadcasted_iota(jnp.int32, (16, 128), 0) % 4
    scale = 128 ** (-0.5)
    nt = (((1,), (1,)), ((), ()))
    for p in range(n):
        c = t ^ ORDER[p]
        s = p % slots
        for cp in fetch(p):
            cp.wait()
        q = msg[c, 0:16, :]
        new_k = msg[c, 16:24, :]
        new_v = msg[c, 24:32, :]
        s1 = lax.dot_general(q, kbuf[s], nt, preferred_element_type=f32) * scale
        s1 = jnp.where(col < table[1, c], s1, neg_fill)
        m1 = jnp.max(s1, axis=1, keepdims=True)
        p1 = jnp.exp(s1 - m1)
        l1 = jnp.sum(p1, axis=1, keepdims=True)
        o1 = jnp.dot(p1.astype(bf16), vbuf[s], preferred_element_type=f32)
        s2 = lax.dot_general(q, new_k, nt, preferred_element_type=f32) * scale
        s2 = jnp.where(col8 <= row8, s2, neg_fill)
        m2 = jnp.max(s2, axis=1, keepdims=True)
        p2 = jnp.exp(s2 - m2)
        l2 = jnp.sum(p2, axis=1, keepdims=True)
        o2 = jnp.dot(p2.astype(bf16), new_v, preferred_element_type=f32)
        top = jnp.maximum(m1, m2)
        e1 = jnp.exp(m1 - top)
        e2 = jnp.exp(m2 - top)
        o = (e1 * o1 + e2 * o2) / (e1 * l1 + e2 * l2)
        o = jnp.where(rowd < table[2, c], o, 0.0)
        for h in range(4):
            att[4 * p : 4 * p + 4, 128 * h : 128 * h + 128] = o[4 * h : 4 * h + 4, :]
        if p + slots < n:
            for cp in fetch(p + slots):
                cp.start()
    wcopy.wait()
    a = att[...].astype(bf16)
    half = a.shape[0] // 2
    width = wbuf.shape[1]
    step = 512
    for k in range(0, width, step):
        y = jnp.dot(a, wbuf[:, k : k + step], preferred_element_type=f32)
        keep[:, k : k + step] = y[:half]
        send[:, k : k + step] = y[half:].astype(bf16)


def attend(table, msg, keys, values, weight):
    n, rows, width = msg.shape
    depth, out_width = weight.shape
    slots = 8
    return pl.pallas_call(
        attend_kernel,
        out_shape=(
            jax.ShapeDtypeStruct((2 * n, out_width), f32),
            jax.ShapeDtypeStruct((2 * n, out_width), bf16),
        ),
        in_specs=[
            pl.BlockSpec(memory_space=pltpu.SMEM),
            pl.BlockSpec(memory_space=pltpu.VMEM),
            pl.BlockSpec(memory_space=pl.ANY),
            pl.BlockSpec(memory_space=pl.ANY),
            pl.BlockSpec(memory_space=pl.ANY),
        ],
        out_specs=(pl.BlockSpec(memory_space=pltpu.VMEM),) * 2,
        scratch_shapes=[
            pltpu.VMEM((4 * n, depth), f32),
            pltpu.VMEM((slots,) + keys.shape[1:], bf16),
            pltpu.VMEM((slots,) + values.shape[1:], bf16),
            pltpu.VMEM((depth, out_width), bf16),
            pltpu.SemaphoreType.DMA((3, slots)),
        ],
        compiler_params=pltpu.CompilerParams(vmem_limit_bytes=32 * 1024 * 1024),
        cost_estimate=pl.CostEstimate(
            flops=4 * n * 16 * 512 * 128 + 2 * 4 * n * depth * out_width,
            bytes_accessed=4 * keys.size + 2 * weight.size,
            transcendentals=0,
        ),
        name="attend",
    )(table, msg, keys, values, weight)


def place_kernel(table, fresh, got, out, rows):
    s = pl.program_id(0)

    @pl.when(s == 0)
    def _():
        rows[...] = fresh[...].astype(f32)

    length = table[3, s]
    rest = table[4, s]
    held = jnp.where(rest > 0, length, 0)
    places = lax.broadcasted_iota(jnp.int32, got.shape[1:], 0)
    block = got[0]
    out[0] = jnp.where(places < held, block, jnp.zeros((), block.dtype))
    start = pl.multiple_of(jnp.minimum(length // 16 * 16, got.shape[1] - 32), 16)
    window = out[0, pl.ds(start, 32), :].astype(f32)
    inner = lax.broadcasted_iota(jnp.int32, window.shape, 0) + start
    for u in range(fresh.shape[0]):
        row = rows[u, pl.ds(s, 1), :]
        window = jnp.where((inner == length + u) & (rest > u), row, window)
    out[0, pl.ds(start, 32), :] = window.astype(bf16)


def place(table, fresh, got):
    n, length, width = got.shape
    return pl.pallas_call(
        place_kernel,
        out_shape=jax.ShapeDtypeStruct(got.shape, got.dtype),
        grid=(n,),
        in_specs=[
            pl.BlockSpec(memory_space=pltpu.SMEM),
            pl.BlockSpec(fresh.shape, lambda i: (0, 0, 0)),
            pl.BlockSpec((1, length, width), lambda i: (i, 0, 0)),
        ],
        out_specs=pl.BlockSpec((1, length, width), lambda i: (i, 0, 0)),
        scratch_shapes=[pltpu.VMEM(fresh.shape, f32)],
        cost_estimate=pl.CostEstimate(
            flops=0, bytes_accessed=4 * got.size, transcendentals=0
        ),
        name="place",
    )(table, fresh, got)


def finish_kernel(table, first, second, third, residual, gain, out, normed, sums, squares):
    t = table[5, 0]
    rows = residual.shape[0]
    row = lax.broadcasted_iota(jnp.int32, (rows, rows), 0)
    col = lax.broadcasted_iota(jnp.int32, (rows, rows), 1)
    i = col // 4
    turned = (i & 1) * 8 + (i // 2 & 1) * 4 + (i // 4 & 1) * 2 + (i // 8 & 1)
    target = (col % 4) * 16 + (t ^ turned)
    pick = jnp.where(row == target, 1.0, 0.0).astype(bf16)
    a, b = first.shape[0], first.shape[0] + second.shape[0]
    step = 512
    total = jnp.zeros((rows, 128), f32)
    for k in range(0, residual.shape[1], step):
        cut = slice(k, k + step)
        piece = jnp.concatenate([first[:, cut], second[:, cut], third[:, cut]], axis=0)
        level = residual[:, cut].astype(f32) + jnp.dot(pick, piece, preferred_element_type=f32)
        out[:, cut] = level.astype(bf16)
        sums[:, cut] = level
        sq = level * level
        for j in range(0, step, 128):
            total = total + sq[:, j : j + 128]
    mean = jnp.sum(total, axis=1, keepdims=True) / residual.shape[1]
    factor = lax.rsqrt(mean + eps)
    for k in range(0, residual.shape[1], step):
        cut = slice(k, k + step)
        normed[:, cut] = (sums[:, cut] * factor * gain[:, cut].astype(f32)).astype(bf16)


def finish(table, first, second, third, residual, gain):
    rows, width = residual.shape
    vm = pl.BlockSpec(memory_space=pltpu.VMEM)
    return pl.pallas_call(
        finish_kernel,
        out_shape=(jax.ShapeDtypeStruct((rows, width), bf16),) * 2,
        in_specs=[pl.BlockSpec(memory_space=pltpu.SMEM)] + [vm] * 5,
        out_specs=(vm, vm),
        scratch_shapes=[pltpu.VMEM((rows, width), f32), pltpu.VMEM((rows, 128), f32)],
        compiler_params=pltpu.CompilerParams(vmem_limit_bytes=16 * 1024 * 1024),
        cost_estimate=pl.CostEstimate(
            flops=2 * rows * rows * width, bytes_accessed=8 * rows * width, transcendentals=0
        ),
        name="finish",
    )(table, first, second, third, residual, gain)


def swap(x, mask):
    return lax.ppermute(x, "tensor", [(t, t ^ mask) for t in range(16)])


def hand_over(x, mask):
    return lax.ppermute(
        x,
        ("group", "tensor"),
        [(g * 16 + t, t * 16 + (g ^ mask)) for g in range(16) for t in range(16)],
    )


def on_device(
    queries,
    new_keys,
    new_values,
    key_cache,
    value_cache,
    cache_len,
    remaining,
    dest_table,
    residual_in,
    out_weight,
    norm_gain,
):
    group = lax.axis_index("group")
    tensor = lax.axis_index("tensor")
    steps, n, heads, width = queries.shape
    out_width = out_weight.shape[1]
    asked = jnp.transpose(queries, (1, 2, 0, 3)).reshape(n, heads * steps, width)
    pad = ((0, 0), (0, 4), (0, 0))
    msg = jnp.concatenate(
        [
            asked,
            jnp.pad(jnp.swapaxes(new_keys[:, :, 0, :], 0, 1), pad),
            jnp.pad(jnp.swapaxes(new_values[:, :, 0, :], 0, 1), pad),
        ],
        axis=1,
    )
    msg = lax.all_to_all(msg, "group", split_axis=0, concat_axis=0, tiled=True)

    numbers = jnp.arange(n, dtype=jnp.int32)
    dest = dest_table.reshape(n, n)
    lens = cache_len.reshape(n, n)
    rest = remaining.reshape(n, n)
    mine = numbers[:, None] == group
    own_dest = jnp.sum(jnp.where(mine, dest, 0), axis=0)
    own_len = jnp.sum(jnp.where(mine, lens, 0), axis=0)
    own_rest = jnp.sum(jnp.where(mine, rest, 0), axis=0)
    goes = own_dest[None, :] // n == numbers[:, None]
    comes = dest == group * n + numbers[:, None]
    table = jnp.stack(
        [
            jnp.sum(jnp.where(goes, numbers[None, :], 0), axis=1),
            jnp.sum(jnp.where(goes, own_len[None, :], 0), axis=1),
            jnp.sum(jnp.where(goes, own_rest[None, :], 0), axis=1),
            jnp.sum(jnp.where(comes, lens, 0), axis=1),
            jnp.sum(jnp.where(comes, rest, 0), axis=1),
            jnp.full((n,), tensor, jnp.int32),
        ]
    )
    keys, values = order_cache(table, key_cache[:, 0], value_cache[:, 0])
    keys_got = lax.all_to_all(keys, "group", split_axis=0, concat_axis=0, tiled=True)
    keep, send = attend(table, msg, keys, values, out_weight)
    s = keep + swap(send, 1).astype(f32)
    s = s[:16] + swap(s[16:].astype(bf16), 2).astype(f32)
    s = s[:8] + swap(s[8:].astype(bf16), 4).astype(f32)
    s = s[:4] + swap(s[4:].astype(bf16), 8).astype(f32)
    s = s.astype(bf16)
    s, values_now = lax.optimization_barrier((s, values))
    values_got = lax.all_to_all(values_now, "group", split_axis=0, concat_axis=0, tiled=True)
    first = jnp.concatenate([hand_over(s, m) for m in (0, 8, 4, 12)], axis=0)
    second = swap(first, 2)
    third = swap(jnp.concatenate([first, second], axis=0), 1)
    residual_out, normed = finish(
        table,
        first,
        second,
        third,
        residual_in.reshape(steps * n, out_width),
        norm_gain.reshape(1, out_width),
    )
    key_out = place(table, new_keys[:, :, 0, :], keys_got)
    value_out = place(table, new_values[:, :, 0, :], values_got)
    return (
        residual_out.reshape(steps, n, out_width),
        normed.reshape(steps, n, out_width),
        key_out[:, None],
        value_out[:, None],
    )


def solution(mesh):
    placed = (
        P(None, "group", "tensor", None),
        P(None, "group", "tensor", None),
        P(None, "group", "tensor", None),
        P("group", "tensor", None, None),
        P("group", "tensor", None, None),
        P(),
        P(),
        P(),
        P(None, "group", None),
        P("tensor", None),
        P(),
    )
    return jax.shard_map(
        on_device,
        mesh=mesh,
        in_specs=placed,
        out_specs=(
            P(None, "group", None),
            P(None, "group", None),
            P("group", "tensor", None, None),
            P("group", "tensor", None, None),
        ),
        check_vma=False,
    )
```

```python
import functools

import jax
import jax.numpy as jnp
from jax import lax
from jax.experimental import pallas as pl
from jax.experimental.pallas import tpu as pltpu
from jax.sharding import PartitionSpec as P

neg_fill = -1e30
eps = 1e-06
ORDER = (0, 8, 4, 12, 2, 10, 6, 14, 1, 9, 5, 13, 3, 11, 7, 15)
f32 = jnp.float32
bf16 = jnp.bfloat16


def ask_kernel(queries, new_keys, new_values, msg, asked, built):
    steps, n, heads, width = queries.shape
    rows = msg.shape[1]
    asked[...] = queries[...].astype(f32).reshape(asked.shape)
    built[...] = jnp.zeros(built.shape, f32)
    for t in range(steps):
        for h in range(heads):
            built[pl.ds(4 * h + t, n, stride=rows), :] = asked[
                pl.ds(t * n * heads + h, n, stride=heads), :
            ]
        built[pl.ds(16 + t, n, stride=rows), :] = new_keys[t].astype(f32)
        built[pl.ds(24 + t, n, stride=rows), :] = new_values[t].astype(f32)
    msg[...] = built[...].astype(bf16).reshape(msg.shape)


def ask(queries, new_keys, new_values):
    steps, n, heads, width = queries.shape
    vm = pl.BlockSpec(memory_space=pltpu.VMEM)
    return pl.pallas_call(
        ask_kernel,
        out_shape=jax.ShapeDtypeStruct((n, 32, width), bf16),
        in_specs=[vm] * 3,
        out_specs=vm,
        scratch_shapes=[
            pltpu.VMEM((steps * n * heads, width), f32),
            pltpu.VMEM((n * 32, width), f32),
        ],
        compiler_params=pltpu.CompilerParams(vmem_limit_bytes=60 * 1024 * 1024),
        cost_estimate=pl.CostEstimate(flops=0, bytes_accessed=400000, transcendentals=0),
        name="ask",
    )(queries, new_keys, new_values)


def order_kernel(dest, lens, rest, keys, values, large, small, table, kbuf, vbuf, sems):
    n, length, _ = keys.shape
    part = length - small.shape[1]
    group = lax.axis_index("group")
    table[5, 0] = lax.axis_index("tensor") ^ group
    for j in range(n):
        d = dest[group * n + j] // n
        table[0, d] = j
        table[1, d] = lens[group * n + j]
        table[2, d] = rest[group * n + j]

    def fetch(d):
        j = table[0, d]
        return (
            pltpu.make_async_copy(keys.at[j], kbuf.at[d], sems.at[0, d]),
            pltpu.make_async_copy(values.at[j], vbuf.at[d], sems.at[1, d]),
        )

    def store(d):
        return (
            pltpu.make_async_copy(kbuf.at[d], large.at[d, pl.ds(0, length)], sems.at[2, d]),
            pltpu.make_async_copy(
                vbuf.at[d, pl.ds(0, part)], large.at[d, pl.ds(length, part)], sems.at[3, d]
            ),
            pltpu.make_async_copy(
                vbuf.at[d, pl.ds(part, length - part)], small.at[d], sems.at[4, d]
            ),
        )

    for d in range(n):
        for c in fetch(d):
            c.start()

    def note(s, _):
        place = s * n
        for j in range(n):
            place = jnp.where(dest[s * n + j] // n == group, s * n + j, place)
        table[3, s] = lens[place]
        table[4, s] = rest[place]
        return 0

    lax.fori_loop(0, n, note, 0)
    for d in range(n):
        for c in fetch(d):
            c.wait()
        for c in store(d):
            c.start()
    for d in range(n):
        for c in store(d):
            c.wait()


def order_cache(dest, lens, rest, keys, values, part):
    n, length, width = keys.shape
    sm = pl.BlockSpec(memory_space=pltpu.SMEM)
    hbm = pl.BlockSpec(memory_space=pl.ANY)
    return pl.pallas_call(
        order_kernel,
        out_shape=(
            jax.ShapeDtypeStruct((n, length + part, width), keys.dtype),
            jax.ShapeDtypeStruct((n, length - part, width), keys.dtype),
            jax.ShapeDtypeStruct((6, n), jnp.int32),
        ),
        in_specs=[sm, sm, sm, hbm, hbm],
        out_specs=(hbm, hbm, sm),
        scratch_shapes=[
            pltpu.VMEM(keys.shape, keys.dtype),
            pltpu.VMEM(values.shape, values.dtype),
            pltpu.SemaphoreType.DMA((5, n)),
        ],
        compiler_params=pltpu.CompilerParams(vmem_limit_bytes=60 * 1024 * 1024),
        cost_estimate=pl.CostEstimate(
            flops=0, bytes_accessed=8 * keys.size, transcendentals=0
        ),
        name="order_cache",
    )(dest, lens, rest, keys, values)


def attend_kernel(turn, table, msg, keys, values, weight, keep, near, far, att, kbuf, vbuf, wbuf, sems):
    t = table[5, 0]
    n = kbuf.shape[0]
    wcopy = pltpu.make_async_copy(weight, wbuf, sems.at[2, 0])

    def fetch(p):
        j = table[0, t ^ ORDER[p]]
        return (
            pltpu.make_async_copy(keys.at[j], kbuf.at[p], sems.at[0, p]),
            pltpu.make_async_copy(values.at[j], vbuf.at[p], sems.at[1, p]),
        )

    for p in range(n):
        for c in fetch(p):
            c.start()
    wcopy.start()
    col = lax.broadcasted_iota(jnp.int32, (16, keys.shape[1]), 1)
    row8 = lax.broadcasted_iota(jnp.int32, (16, 8), 0) % 4
    col8 = lax.broadcasted_iota(jnp.int32, (16, 8), 1)
    rowd = lax.broadcasted_iota(jnp.int32, (16, 128), 0) % 4
    scale = 128 ** (-0.5)
    nt = (((1,), (1,)), ((), ()))
    batch = 4
    for start in range(0, n, batch):
        ps = range(start, start + batch)
        for p in ps:
            for cp in fetch(p):
                cp.wait()
        cs = [t ^ ORDER[p] for p in ps]
        qs = [msg[c, 0:16, :] for c in cs]
        nks = [msg[c, 16:24, :] for c in cs]
        nvs = [msg[c, 24:32, :] for c in cs]
        s1 = [lax.dot_general(q, kbuf[p], nt, preferred_element_type=f32) for q, p in zip(qs, ps)]
        s2 = [lax.dot_general(q, k, nt, preferred_element_type=f32) for q, k in zip(qs, nks)]
        s1 = [jnp.where(col < table[1, c], s * scale, neg_fill) for s, c in zip(s1, cs)]
        s2 = [jnp.where(col8 <= row8, s * scale, neg_fill) for s in s2]
        m1 = [jnp.max(s, axis=1, keepdims=True) for s in s1]
        m2 = [jnp.max(s, axis=1, keepdims=True) for s in s2]
        p1 = [jnp.exp(s - m) for s, m in zip(s1, m1)]
        p2 = [jnp.exp(s - m) for s, m in zip(s2, m2)]
        o1 = [
            jnp.dot(w.astype(bf16), vbuf[p], preferred_element_type=f32) for w, p in zip(p1, ps)
        ]
        o2 = [
            jnp.dot(w.astype(bf16), v, preferred_element_type=f32) for w, v in zip(p2, nvs)
        ]
        l1 = [jnp.sum(w, axis=1, keepdims=True) for w in p1]
        l2 = [jnp.sum(w, axis=1, keepdims=True) for w in p2]
        for i, p in enumerate(ps):
            top = jnp.maximum(m1[i], m2[i])
            e1 = jnp.exp(m1[i] - top)
            e2 = jnp.exp(m2[i] - top)
            o = (e1 * o1[i] + e2 * o2[i]) / (e1 * l1[i] + e2 * l2[i])
            o = jnp.where(rowd < table[2, cs[i]], o, 0.0)
            for h in range(4):
                att[4 * p : 4 * p + 4, 128 * h : 128 * h + 128] = o[4 * h : 4 * h + 4, :]
    wcopy.wait()
    a = att[...].astype(bf16)
    rows = a.shape[0]
    width = wbuf.shape[1]
    step = 512
    for k in range(0, width, step):
        y = jnp.dot(a, wbuf[:, k : k + step], preferred_element_type=f32)
        keep[:, k : k + step] = y[: rows // 2]
        near[:, k : k + step] = y[rows // 2 : rows * 3 // 4].astype(bf16)
        far[:, k : k + step] = y[rows * 3 // 4 :].astype(bf16)


def attend(turn, table, msg, keys, values, weight):
    n = msg.shape[0]
    depth, out_width = weight.shape
    vm = pl.BlockSpec(memory_space=pltpu.VMEM)
    sm = pl.BlockSpec(memory_space=pltpu.SMEM)
    hbm = pl.BlockSpec(memory_space=pl.ANY)
    return pl.pallas_call(
        attend_kernel,
        out_shape=(
            jax.ShapeDtypeStruct((2 * n, out_width), f32),
            jax.ShapeDtypeStruct((n, out_width), bf16),
            jax.ShapeDtypeStruct((n, out_width), bf16),
        ),
        in_specs=[sm, sm, vm, hbm, hbm, hbm],
        out_specs=(vm, vm, vm),
        scratch_shapes=[
            pltpu.VMEM((4 * n, depth), f32),
            pltpu.VMEM(keys.shape, bf16),
            pltpu.VMEM(values.shape, bf16),
            pltpu.VMEM((depth, out_width), bf16),
            pltpu.SemaphoreType.DMA((3, n)),
        ],
        compiler_params=pltpu.CompilerParams(vmem_limit_bytes=48 * 1024 * 1024),
        cost_estimate=pl.CostEstimate(
            flops=4 * n * 16 * 512 * 128 + 2 * 4 * n * depth * out_width,
            bytes_accessed=4 * keys.size + 2 * weight.size,
            transcendentals=0,
        ),
        name="attend",
    )(turn, table, msg, keys, values, weight)


def place_kernel(table, fresh, *refs):
    *got, out, rows = refs
    count, total, _ = out.shape

    @pl.when(pl.program_id(0) == 0)
    def _():
        rows[...] = fresh[...].astype(f32)

    slots = [pl.program_id(0) * count + b for b in range(count)]
    lengths = [table[3, s] for s in slots]
    rests = [table[4, s] for s in slots]
    helds = [jnp.where(r > 0, l, 0) for l, r in zip(lengths, rests)]
    step = 32
    for b in range(count):
        base = 0
        for piece in got:
            for k in range(0, piece.shape[1], step):
                block = piece[b, k : k + step, :]
                out[b, base : base + step, :] = jnp.where(
                    base < helds[b], block, jnp.zeros((), block.dtype)
                )
                base += step
    starts = [pl.multiple_of(jnp.minimum(l // 16 * 16, total - 32), 16) for l in lengths]
    windows = [out[b, pl.ds(start, 32), :].astype(f32) for b, start in enumerate(starts)]
    news = [[rows[u, pl.ds(s, 1), :] for u in range(fresh.shape[0])] for s in slots]
    place_in = lax.broadcasted_iota(jnp.int32, windows[0].shape, 0)
    for b in range(count):
        inner = place_in + starts[b]
        window = jnp.where(inner < helds[b], windows[b], 0.0)
        for u, row in enumerate(news[b]):
            spot = jnp.where(rests[b] > u, lengths[b] + u, -1)
            window = jnp.where(inner == spot, row, window)
        windows[b] = window.astype(bf16)
    for b, start in enumerate(starts):
        out[b, pl.ds(start, 32), :] = windows[b]


def place(table, fresh, *pieces):
    n, _, width = pieces[0][0].shape
    length = sum(rows for _, _, rows in pieces)
    count = 4
    return pl.pallas_call(
        place_kernel,
        out_shape=jax.ShapeDtypeStruct((n, length, width), bf16),
        grid=(n // count,),
        in_specs=[
            pl.BlockSpec(memory_space=pltpu.SMEM),
            pl.BlockSpec(fresh.shape, lambda i: (0, 0, 0)),
        ]
        + [
            pl.BlockSpec((count, rows, width), functools.partial(lambda k, i: (i, k, 0), first // rows))
            for _, first, rows in pieces
        ],
        out_specs=pl.BlockSpec((count, length, width), lambda i: (i, 0, 0)),
        scratch_shapes=[pltpu.VMEM(fresh.shape, f32)],
        compiler_params=pltpu.CompilerParams(vmem_limit_bytes=8 * 1024 * 1024),
        cost_estimate=pl.CostEstimate(
            flops=0, bytes_accessed=4 * n * length * width, transcendentals=0
        ),
        name="place",
    )(table, fresh, *[array for array, _, _ in pieces])


def finish_kernel(table, first, second, third, fourth, residual, gain, out, normed, sums, squares):
    t = table[5, 0]
    rows = residual.shape[0]
    row = lax.broadcasted_iota(jnp.int32, (rows, rows), 0)
    col = lax.broadcasted_iota(jnp.int32, (rows, rows), 1)
    i = col // 4
    turned = (i & 1) * 8 + (i // 2 & 1) * 4 + (i // 4 & 1) * 2 + (i // 8 & 1)
    target = (col % 4) * 16 + (t ^ turned)
    pick = jnp.where(row == target, 1.0, 0.0).astype(bf16)
    step = 512
    total = jnp.zeros((rows, 128), f32)
    for k in range(0, residual.shape[1], step):
        cut = slice(k, k + step)
        piece = jnp.concatenate([x[:, cut] for x in (first, second, third, fourth)], axis=0)
        level = residual[:, cut].astype(f32) + jnp.dot(pick, piece, preferred_element_type=f32)
        out[:, cut] = level.astype(bf16)
        sums[:, cut] = level
        sq = level * level
        for j in range(0, step, 128):
            total = total + sq[:, j : j + 128]
    mean = jnp.sum(total, axis=1, keepdims=True) / residual.shape[1]
    factor = lax.rsqrt(mean + eps)
    for k in range(0, residual.shape[1], step):
        cut = slice(k, k + step)
        normed[:, cut] = (sums[:, cut] * factor * gain[:, cut].astype(f32)).astype(bf16)


def finish(table, first, second, third, fourth, residual, gain):
    rows, width = residual.shape
    vm = pl.BlockSpec(memory_space=pltpu.VMEM)
    return pl.pallas_call(
        finish_kernel,
        out_shape=(jax.ShapeDtypeStruct((rows, width), bf16),) * 2,
        in_specs=[pl.BlockSpec(memory_space=pltpu.SMEM)] + [vm] * 6,
        out_specs=(vm, vm),
        scratch_shapes=[pltpu.VMEM((rows, width), f32), pltpu.VMEM((rows, 128), f32)],
        compiler_params=pltpu.CompilerParams(vmem_limit_bytes=16 * 1024 * 1024),
        cost_estimate=pl.CostEstimate(
            flops=2 * rows * rows * width, bytes_accessed=8 * rows * width, transcendentals=0
        ),
        name="finish",
    )(table, first, second, third, fourth, residual, gain)


def swap(x, mask):
    return lax.ppermute(x, "tensor", [(t, t ^ mask) for t in range(16)])


def hand_over(x, mask):
    return lax.ppermute(
        x,
        ("group", "tensor"),
        [(g * 16 + t, (g ^ t) * 16 + (t ^ mask)) for g in range(16) for t in range(16)],
    )


def on_device(
    queries,
    new_keys,
    new_values,
    key_cache,
    value_cache,
    cache_len,
    remaining,
    dest_table,
    residual_in,
    out_weight,
    norm_gain,
):
    steps, n, heads, width = queries.shape
    out_width = out_weight.shape[1]
    fresh_keys = new_keys[:, :, 0, :]
    fresh_values = new_values[:, :, 0, :]
    msg = ask(queries, fresh_keys, fresh_values)
    msg = lax.all_to_all(msg, "group", split_axis=0, concat_axis=0, tiled=True)
    old_keys, old_values = key_cache[:, 0], value_cache[:, 0]
    part = 64
    large, small, table = order_cache(
        dest_table, cache_len, remaining, old_keys, old_values, part
    )
    large = lax.all_to_all(large, "group", split_axis=0, concat_axis=0, tiled=True)

    def first_steps(turn):
        keep, near, far = attend(turn[None], table, msg, old_keys, old_values, out_weight)
        far, near = swap(far, 1), swap(near, 1)
        s = keep[16:] + far.astype(f32)
        s = keep[:16] + near.astype(f32) + swap(s.astype(bf16), 2).astype(f32)
        s = s[:8] + swap(s[8:].astype(bf16), 4).astype(f32)
        return s[:4], s[4:].astype(bf16)

    def no_steps(turn):
        return jnp.zeros((4, out_width), f32), jnp.zeros((4, out_width), bf16)

    tensor = lax.axis_index("tensor")
    s, send = lax.cond(tensor >= 0, first_steps, no_steps, tensor)
    s, send, large = lax.optimization_barrier((s, send, large))
    s = s + swap(send, 8).astype(f32)
    s = s.astype(bf16)
    first = jnp.concatenate([hand_over(s, m) for m in (0, 8)], axis=0)
    first, small = lax.optimization_barrier((first, small))
    small = lax.all_to_all(small, "group", split_axis=0, concat_axis=0, tiled=True)
    first = jnp.concatenate([first, swap(first, 4)], axis=0)
    second = swap(first, 2)
    third = swap(first, 1)
    fourth = swap(second, 1)
    length = old_keys.shape[1]
    key_out = place(table, fresh_keys, (large, 0, length))
    value_out = place(table, fresh_values, (large, length, part), (small, 0, length - part))
    fourth, value_out = lax.optimization_barrier((fourth, value_out))
    residual_out, normed = finish(
        table,
        first,
        second,
        third,
        fourth,
        residual_in.reshape(steps * n, out_width),
        norm_gain.reshape(1, out_width),
    )
    return (
        residual_out.reshape(steps, n, out_width),
        normed.reshape(steps, n, out_width),
        key_out[:, None],
        value_out[:, None],
    )


def solution(mesh):
    placed = (
        P(None, "group", "tensor", None),
        P(None, "group", "tensor", None),
        P(None, "group", "tensor", None),
        P("group", "tensor", None, None),
        P("group", "tensor", None, None),
        P(),
        P(),
        P(),
        P(None, "group", None),
        P("tensor", None),
        P(),
    )
    return jax.shard_map(
        on_device,
        mesh=mesh,
        in_specs=placed,
        out_specs=(
            P(None, "group", None),
            P(None, "group", None),
            P("group", "tensor", None, None),
            P("group", "tensor", None, None),
        ),
        check_vma=False,
    )
```

```python
import functools

import jax
import jax.numpy as jnp
from jax import lax
from jax.experimental import pallas as pl
from jax.experimental.pallas import tpu as pltpu
from jax.sharding import PartitionSpec as P

neg_fill = -1e30
eps = 1e-06
ORDER = (0, 8, 4, 12, 2, 10, 6, 14, 1, 9, 5, 13, 3, 11, 7, 15)
f32 = jnp.float32
bf16 = jnp.bfloat16


def ask_kernel(queries, new_keys, new_values, msg, asked, built):
    steps, n, heads, width = queries.shape
    rows = msg.shape[1]
    asked[...] = queries[...].astype(f32).reshape(asked.shape)
    built[...] = jnp.zeros(built.shape, f32)
    for t in range(steps):
        for h in range(heads):
            built[pl.ds(4 * h + t, n, stride=rows), :] = asked[
                pl.ds(t * n * heads + h, n, stride=heads), :
            ]
        built[pl.ds(16 + t, n, stride=rows), :] = new_keys[t].astype(f32)
        built[pl.ds(24 + t, n, stride=rows), :] = new_values[t].astype(f32)
    msg[...] = built[...].astype(bf16).reshape(msg.shape)


def ask(queries, new_keys, new_values):
    steps, n, heads, width = queries.shape
    vm = pl.BlockSpec(memory_space=pltpu.VMEM)
    return pl.pallas_call(
        ask_kernel,
        out_shape=jax.ShapeDtypeStruct((n, 32, width), bf16),
        in_specs=[vm] * 3,
        out_specs=vm,
        scratch_shapes=[
            pltpu.VMEM((steps * n * heads, width), f32),
            pltpu.VMEM((n * 32, width), f32),
        ],
        compiler_params=pltpu.CompilerParams(vmem_limit_bytes=60 * 1024 * 1024),
        cost_estimate=pl.CostEstimate(flops=0, bytes_accessed=400000, transcendentals=0),
        name="ask",
    )(queries, new_keys, new_values)


def fold(t):
    return t ^ (3 * (t // 4 % 2))


def order_kernel(dest, lens, rest, keys, values, large, small, table, kbuf, vbuf, sems):
    n, length, _ = keys.shape
    part = length - small.shape[1]
    rest_rows = large.shape[1] - part
    share = length - rest_rows
    both = length - 2 * share
    group = lax.axis_index("group")
    tensor = lax.axis_index("tensor")
    table[5, 0] = fold(tensor) ^ group
    table[5, 1] = tensor & 1
    base = pl.multiple_of((tensor & 1) * share, 16)
    for j in range(n):
        d = dest[group * n + j] // n
        table[0, d] = j
        table[1, d] = lens[group * n + j]
        table[2, d] = rest[group * n + j]

    def fetch(d):
        j = table[0, d]
        return (
            pltpu.make_async_copy(
                keys.at[j, pl.ds(base, share)], kbuf.at[d, pl.ds(0, share)], sems.at[0, d]
            ),
            pltpu.make_async_copy(
                keys.at[j, pl.ds(2 * share, both)], kbuf.at[d, pl.ds(share, both)], sems.at[5, d]
            ),
            pltpu.make_async_copy(values.at[j], vbuf.at[d], sems.at[1, d]),
        )

    def store(d):
        return (
            pltpu.make_async_copy(kbuf.at[d], large.at[d, pl.ds(part, rest_rows)], sems.at[2, d]),
            pltpu.make_async_copy(
                vbuf.at[d, pl.ds(0, part)], large.at[d, pl.ds(0, part)], sems.at[3, d]
            ),
            pltpu.make_async_copy(
                vbuf.at[d, pl.ds(part, length - part)], small.at[d], sems.at[4, d]
            ),
        )

    for d in range(n):
        for c in fetch(d):
            c.start()

    def note(s, _):
        place = s * n
        for j in range(n):
            place = jnp.where(dest[s * n + j] // n == group, s * n + j, place)
        table[3, s] = lens[place]
        table[4, s] = rest[place]
        return 0

    lax.fori_loop(0, n, note, 0)
    for d in range(n):
        for c in fetch(d):
            c.wait()
        for c in store(d):
            c.start()
    for d in range(n):
        for c in store(d):
            c.wait()


def order_cache(dest, lens, rest, keys, values, part, share):
    n, length, width = keys.shape
    sm = pl.BlockSpec(memory_space=pltpu.SMEM)
    hbm = pl.BlockSpec(memory_space=pl.ANY)
    return pl.pallas_call(
        order_kernel,
        out_shape=(
            jax.ShapeDtypeStruct((n, part + length - share, width), keys.dtype),
            jax.ShapeDtypeStruct((n, length - part, width), keys.dtype),
            jax.ShapeDtypeStruct((6, n), jnp.int32),
        ),
        in_specs=[sm, sm, sm, hbm, hbm],
        out_specs=(hbm, hbm, sm),
        scratch_shapes=[
            pltpu.VMEM((n, length - share, width), keys.dtype),
            pltpu.VMEM(values.shape, values.dtype),
            pltpu.SemaphoreType.DMA((6, n)),
        ],
        compiler_params=pltpu.CompilerParams(vmem_limit_bytes=60 * 1024 * 1024),
        cost_estimate=pl.CostEstimate(
            flops=0, bytes_accessed=8 * keys.size, transcendentals=0
        ),
        name="order_cache",
    )(dest, lens, rest, keys, values)


def attend_kernel(turn, table, msg, keys, values, weight, keep, near, far, att, kbuf, vbuf, wbuf, sems):
    t = table[5, 0]
    n = kbuf.shape[0]
    width = wbuf.shape[1]
    chunk = width // 5

    def fetch_weight(k):
        cut = pl.ds(k * chunk, chunk)
        return pltpu.make_async_copy(weight.at[:, cut], wbuf.at[:, cut], sems.at[2, k])


    def fetch(p):
        j = table[0, t ^ ORDER[p]]
        return (
            pltpu.make_async_copy(keys.at[j], kbuf.at[p], sems.at[0, p]),
            pltpu.make_async_copy(values.at[j], vbuf.at[p], sems.at[1, p]),
        )

    for p in range(n):
        for c in fetch(p):
            c.start()
    for k in range(5):
        fetch_weight(k).start()
    col = lax.broadcasted_iota(jnp.int32, (16, keys.shape[1]), 1)
    row8 = lax.broadcasted_iota(jnp.int32, (16, 8), 0) % 4
    col8 = lax.broadcasted_iota(jnp.int32, (16, 8), 1)
    rowd = lax.broadcasted_iota(jnp.int32, (16, 128), 0) % 4
    scale = 128 ** (-0.5)
    nt = (((1,), (1,)), ((), ()))
    batch = 4
    for start in range(0, n, batch):
        ps = range(start, start + batch)
        for p in ps:
            for cp in fetch(p):
                cp.wait()
        cs = [t ^ ORDER[p] for p in ps]
        qs = [msg[c, 0:16, :] for c in cs]
        nks = [msg[c, 16:24, :] for c in cs]
        nvs = [msg[c, 24:32, :] for c in cs]
        s1 = [lax.dot_general(q, kbuf[p], nt, preferred_element_type=f32) for q, p in zip(qs, ps)]
        s2 = [lax.dot_general(q, k, nt, preferred_element_type=f32) for q, k in zip(qs, nks)]
        s1 = [jnp.where(col < table[1, c], s * scale, neg_fill) for s, c in zip(s1, cs)]
        s2 = [jnp.where(col8 <= row8, s * scale, neg_fill) for s in s2]
        m1 = [jnp.max(s, axis=1, keepdims=True) for s in s1]
        m2 = [jnp.max(s, axis=1, keepdims=True) for s in s2]
        p1 = [jnp.exp(s - m) for s, m in zip(s1, m1)]
        p2 = [jnp.exp(s - m) for s, m in zip(s2, m2)]
        o1 = [
            jnp.dot(w.astype(bf16), vbuf[p], preferred_element_type=f32) for w, p in zip(p1, ps)
        ]
        o2 = [
            jnp.dot(w.astype(bf16), v, preferred_element_type=f32) for w, v in zip(p2, nvs)
        ]
        l1 = [jnp.sum(w, axis=1, keepdims=True) for w in p1]
        l2 = [jnp.sum(w, axis=1, keepdims=True) for w in p2]
        for i, p in enumerate(ps):
            top = jnp.maximum(m1[i], m2[i])
            e1 = jnp.exp(m1[i] - top)
            e2 = jnp.exp(m2[i] - top)
            o = (e1 * o1[i] + e2 * o2[i]) / (e1 * l1[i] + e2 * l2[i])
            o = jnp.where(rowd < table[2, cs[i]], o, 0.0)
            for h in range(4):
                att[4 * p : 4 * p + 4, 128 * h : 128 * h + 128] = o[4 * h : 4 * h + 4, :]
    a = att[...].astype(bf16)
    rows = a.shape[0]
    step = 512
    for k in range(0, width, step):
        if k % chunk == 0:
            fetch_weight(k // chunk).wait()
        y = jnp.dot(a, wbuf[:, k : k + step], preferred_element_type=f32)
        keep[:, k : k + step] = y[: rows // 2]
        near[:, k : k + step] = y[rows // 2 : rows * 7 // 8].astype(bf16)
        far[:, k : k + step] = y[rows * 7 // 8 :].astype(bf16)


def attend(turn, table, msg, keys, values, weight):
    n = msg.shape[0]
    depth, out_width = weight.shape
    vm = pl.BlockSpec(memory_space=pltpu.VMEM)
    sm = pl.BlockSpec(memory_space=pltpu.SMEM)
    hbm = pl.BlockSpec(memory_space=pl.ANY)
    return pl.pallas_call(
        attend_kernel,
        out_shape=(
            jax.ShapeDtypeStruct((2 * n, out_width), f32),
            jax.ShapeDtypeStruct((n * 3 // 2, out_width), bf16),
            jax.ShapeDtypeStruct((n // 2, out_width), bf16),
        ),
        in_specs=[sm, sm, vm, hbm, hbm, hbm],
        out_specs=(vm, vm, vm),
        scratch_shapes=[
            pltpu.VMEM((4 * n, depth), f32),
            pltpu.VMEM(keys.shape, bf16),
            pltpu.VMEM(values.shape, bf16),
            pltpu.VMEM((depth, out_width), bf16),
            pltpu.SemaphoreType.DMA((3, n)),
        ],
        compiler_params=pltpu.CompilerParams(vmem_limit_bytes=48 * 1024 * 1024),
        cost_estimate=pl.CostEstimate(
            flops=4 * n * 16 * 512 * 128 + 2 * 4 * n * depth * out_width,
            bytes_accessed=4 * keys.size + 2 * weight.size,
            transcendentals=0,
        ),
        name="attend",
    )(turn, table, msg, keys, values, weight)


def place_kernel(bases, table, fresh, *refs):
    *got, out, rows = refs
    count, total, _ = out.shape

    @pl.when(pl.program_id(0) == 0)
    def _():
        rows[...] = fresh[...].astype(f32)

    slots = [pl.program_id(0) * count + b for b in range(count)]
    lengths = [table[3, s] for s in slots]
    rests = [table[4, s] for s in slots]
    helds = [jnp.where(r > 0, l, 0) for l, r in zip(lengths, rests)]
    step = 32
    for b in range(count):
        for piece, (even, odd) in zip(got, bases):
            base = even
            if odd != even:
                base = pl.multiple_of(even + table[5, 1] * (odd - even), 16)
            for k in range(0, piece.shape[1], step):
                size = min(step, piece.shape[1] - k)
                block = piece[b, k : k + size, :]
                out[b, pl.ds(base + k, size), :] = jnp.where(
                    base + k < helds[b], block, jnp.zeros((), block.dtype)
                )
    starts = [pl.multiple_of(jnp.minimum(l // 16 * 16, total - 32), 16) for l in lengths]
    windows = [out[b, pl.ds(start, 32), :].astype(f32) for b, start in enumerate(starts)]
    news = [[rows[u, pl.ds(s, 1), :] for u in range(fresh.shape[0])] for s in slots]
    place_in = lax.broadcasted_iota(jnp.int32, windows[0].shape, 0)
    for b in range(count):
        inner = place_in + starts[b]
        window = jnp.where(inner < helds[b], windows[b], 0.0)
        for u, row in enumerate(news[b]):
            spot = jnp.where(rests[b] > u, lengths[b] + u, -1)
            window = jnp.where(inner == spot, row, window)
        windows[b] = window.astype(bf16)
    for b, start in enumerate(starts):
        out[b, pl.ds(start, 32), :] = windows[b]


def place(table, fresh, *pieces):
    n, _, width = pieces[0][0].shape
    length = sum(rows for _, _, rows, _ in pieces)
    count = 4
    return pl.pallas_call(
        functools.partial(place_kernel, tuple(bases for _, _, _, bases in pieces)),
        out_shape=jax.ShapeDtypeStruct((n, length, width), bf16),
        grid=(n // count,),
        in_specs=[
            pl.BlockSpec(memory_space=pltpu.SMEM),
            pl.BlockSpec(fresh.shape, lambda i: (0, 0, 0)),
        ]
        + [
            pl.BlockSpec((count, rows, width), functools.partial(lambda k, i: (i, k, 0), start // rows))
            for _, start, rows, _ in pieces
        ],
        out_specs=pl.BlockSpec((count, length, width), lambda i: (i, 0, 0)),
        scratch_shapes=[pltpu.VMEM(fresh.shape, f32)],
        compiler_params=pltpu.CompilerParams(vmem_limit_bytes=62 * 1024 * 1024),
        cost_estimate=pl.CostEstimate(
            flops=0, bytes_accessed=4 * n * length * width, transcendentals=0
        ),
        name="place",
    )(table, fresh, *[array for array, _, _, _ in pieces])


def finish_kernel(table, *refs):
    *pieces, residual, gain, out, normed, sums = refs
    t = table[5, 0]
    rows = residual.shape[0]
    row = lax.broadcasted_iota(jnp.int32, (rows, rows), 0)
    col = lax.broadcasted_iota(jnp.int32, (rows, rows), 1)
    i = col // 4
    turned = (i & 1) * 8 + (i // 2 & 1) * 4 + (i // 4 & 1) * 2 + (i // 8 & 1)
    target = (col % 4) * 16 + (t ^ turned)
    pick = jnp.where(row == target, 1.0, 0.0).astype(bf16)
    step = 512
    total = jnp.zeros((rows, 128), f32)
    for k in range(0, residual.shape[1], step):
        cut = slice(k, k + step)
        piece = jnp.concatenate([x[:, cut].astype(f32) for x in pieces], axis=0).astype(bf16)
        level = residual[:, cut].astype(f32) + jnp.dot(pick, piece, preferred_element_type=f32)
        out[:, cut] = level.astype(bf16)
        sums[:, cut] = level
        sq = level * level
        for j in range(0, step, 128):
            total = total + sq[:, j : j + 128]
    mean = jnp.sum(total, axis=1, keepdims=True) / residual.shape[1]
    factor = lax.rsqrt(mean + eps)
    for k in range(0, residual.shape[1], step):
        cut = slice(k, k + step)
        normed[:, cut] = (sums[:, cut] * factor * gain[:, cut].astype(f32)).astype(bf16)


def finish(table, pieces, residual, gain):
    rows, width = residual.shape
    vm = pl.BlockSpec(memory_space=pltpu.VMEM)
    return pl.pallas_call(
        finish_kernel,
        out_shape=(jax.ShapeDtypeStruct((rows, width), bf16),) * 2,
        in_specs=[pl.BlockSpec(memory_space=pltpu.SMEM)] + [vm] * (len(pieces) + 2),
        out_specs=(vm, vm),
        scratch_shapes=[pltpu.VMEM((rows, width), f32)],
        compiler_params=pltpu.CompilerParams(vmem_limit_bytes=16 * 1024 * 1024),
        cost_estimate=pl.CostEstimate(
            flops=2 * rows * rows * width, bytes_accessed=8 * rows * width, transcendentals=0
        ),
        name="finish",
    )(table, *pieces, residual, gain)


def swap(x, mask):
    return lax.ppermute(x, "tensor", [(t, fold(fold(t) ^ mask)) for t in range(16)])


def hand_over(x, mask):
    return lax.ppermute(
        x,
        ("group", "tensor"),
        [
            (g * 16 + t, (g ^ fold(t)) * 16 + fold(fold(t) ^ mask))
            for g in range(16)
            for t in range(16)
        ],
    )


def on_device(
    queries,
    new_keys,
    new_values,
    key_cache,
    value_cache,
    cache_len,
    remaining,
    dest_table,
    residual_in,
    out_weight,
    norm_gain,
):
    steps, n, heads, width = queries.shape
    out_width = out_weight.shape[1]
    fresh_keys = new_keys[:, :, 0, :]
    fresh_values = new_values[:, :, 0, :]
    msg = ask(queries, fresh_keys, fresh_values)
    msg = lax.all_to_all(msg, "group", split_axis=0, concat_axis=0, tiled=True)
    old_keys, old_values = key_cache[:, 0], value_cache[:, 0]
    length = old_keys.shape[1]
    part, share = 144, 176
    both = length - 2 * share
    large, small, table = order_cache(
        dest_table, cache_len, remaining, old_keys, old_values, part, share
    )
    large = lax.all_to_all(large, "group", split_axis=0, concat_axis=0, tiled=True)

    def first_steps(turn):
        keep, near, far = attend(turn[None], table, msg, old_keys, old_values, out_weight)
        far, near = swap(far, 1), swap(near, 1).astype(f32)
        far = swap((keep[24:] + far.astype(f32)).astype(bf16), 2)
        mid = swap((keep[16:24] + near[16:]).astype(bf16), 2)
        far = swap((keep[8:16] + near[8:16] + far.astype(f32)).astype(bf16), 4)
        s = keep[:8] + near[:8] + mid.astype(f32) + far.astype(f32)
        return s[:4], s[4:].astype(bf16)

    def no_steps(turn):
        return jnp.zeros((4, out_width), f32), jnp.zeros((4, out_width), bf16)

    tensor = lax.axis_index("tensor")
    s, send = lax.cond(tensor >= 0, first_steps, no_steps, tensor)
    s, send, large = lax.optimization_barrier((s, send, large))
    key_share = large[:, part : part + share]
    key_other = swap(key_share, 1)

    def next_steps(s, send):
        s = (s + swap(send, 8).astype(f32)).astype(bf16)
        return jnp.concatenate([hand_over(s, m) for m in (0, 8)], axis=0)

    first = lax.cond(
        tensor >= 0,
        next_steps,
        lambda s, send: jnp.zeros((8, out_width), bf16),
        s,
        send,
    )
    first, small = lax.optimization_barrier((first, small))
    by4 = swap(first, 4)
    by2 = swap(first, 2)
    by1 = swap(first, 1)
    small = lax.all_to_all(small, "group", split_axis=0, concat_axis=0, tiled=True)
    key_out = place(
        table,
        fresh_keys,
        (large, part + share, both, (2 * share, 2 * share)),
        (key_share, 0, share, (0, share)),
        (key_other, 0, share, (share, 0)),
    )
    by4, key_out = lax.optimization_barrier((by4, key_out))
    by42 = swap(by4, 2)
    later = swap(jnp.concatenate([by4, by2], axis=0), 1)
    by42, by1 = lax.optimization_barrier((by42, by1))
    last = swap(by42, 1)
    value_out = place(
        table,
        fresh_values,
        (large, 0, part, (0, 0)),
        (small, 0, length - part, (part, part)),
    )
    last, value_out = lax.optimization_barrier((last, value_out))
    residual_out, normed = finish(
        table,
        (first, by4, by2, by42, by1, later, last),
        residual_in.reshape(steps * n, out_width),
        norm_gain.reshape(1, out_width),
    )
    return (
        residual_out.reshape(steps, n, out_width),
        normed.reshape(steps, n, out_width),
        key_out[:, None],
        value_out[:, None],
    )


def solution(mesh):
    placed = (
        P(None, "group", "tensor", None),
        P(None, "group", "tensor", None),
        P(None, "group", "tensor", None),
        P("group", "tensor", None, None),
        P("group", "tensor", None, None),
        P(),
        P(),
        P(),
        P(None, "group", None),
        P("tensor", None),
        P(),
    )
    return jax.shard_map(
        on_device,
        mesh=mesh,
        in_specs=placed,
        out_specs=(
            P(None, "group", None),
            P(None, "group", None),
            P("group", "tensor", None, None),
            P("group", "tensor", None, None),
        ),
        check_vma=False,
    )
```

```python
import functools

import jax
import jax.numpy as jnp
from jax import lax
from jax.experimental import pallas as pl
from jax.experimental.pallas import tpu as pltpu
from jax.sharding import PartitionSpec as P

neg_fill = -1e30
eps = 1e-06
ORDER = (0, 8, 4, 12, 2, 10, 6, 14, 1, 9, 5, 13, 3, 11, 7, 15)
f32 = jnp.float32
bf16 = jnp.bfloat16


def ask_kernel(queries, new_keys, new_values, msg, asked, built):
    steps, n, heads, width = queries.shape
    rows = msg.shape[1]
    asked[...] = queries[...].astype(f32).reshape(asked.shape)
    built[...] = jnp.zeros(built.shape, f32)
    for t in range(steps):
        for h in range(heads):
            built[pl.ds(4 * h + t, n, stride=rows), :] = asked[
                pl.ds(t * n * heads + h, n, stride=heads), :
            ]
        built[pl.ds(16 + t, n, stride=rows), :] = new_keys[t].astype(f32)
        built[pl.ds(24 + t, n, stride=rows), :] = new_values[t].astype(f32)
    msg[...] = built[...].astype(bf16).reshape(msg.shape)


def ask(queries, new_keys, new_values):
    steps, n, heads, width = queries.shape
    vm = pl.BlockSpec(memory_space=pltpu.VMEM)
    return pl.pallas_call(
        ask_kernel,
        out_shape=jax.ShapeDtypeStruct((n, 32, width), bf16),
        in_specs=[vm] * 3,
        out_specs=vm,
        scratch_shapes=[
            pltpu.VMEM((steps * n * heads, width), f32),
            pltpu.VMEM((n * 32, width), f32),
        ],
        compiler_params=pltpu.CompilerParams(vmem_limit_bytes=60 * 1024 * 1024),
        cost_estimate=pl.CostEstimate(flops=0, bytes_accessed=400000, transcendentals=0),
        name="ask",
    )(queries, new_keys, new_values)


def fold(t):
    return t ^ (3 * (t // 4 % 2))


def order_kernel(dest, lens, rest, keys, values, large, small, table, kbuf, vbuf, sems):
    n, length, _ = keys.shape
    part = length - small.shape[1]
    share = large.shape[1] - part
    group = lax.axis_index("group")
    tensor = lax.axis_index("tensor")
    table[5, 0] = fold(tensor) ^ group
    table[5, 1] = tensor & 1
    base = pl.multiple_of((tensor & 1) * share, 16)
    for j in range(n):
        d = dest[group * n + j] // n
        table[0, d] = j
        table[1, d] = lens[group * n + j]
        table[2, d] = rest[group * n + j]

    def fetch(d):
        j = table[0, d]
        return (
            pltpu.make_async_copy(
                keys.at[j, pl.ds(base, share)], kbuf.at[d], sems.at[0, d]
            ),
            pltpu.make_async_copy(values.at[j], vbuf.at[d], sems.at[1, d]),
        )

    def store(d):
        return (
            pltpu.make_async_copy(kbuf.at[d], large.at[d, pl.ds(part, share)], sems.at[2, d]),
            pltpu.make_async_copy(
                vbuf.at[d, pl.ds(0, part)], large.at[d, pl.ds(0, part)], sems.at[3, d]
            ),
            pltpu.make_async_copy(
                vbuf.at[d, pl.ds(part, length - part)], small.at[d], sems.at[4, d]
            ),
        )

    for d in range(n):
        for c in fetch(d):
            c.start()

    def note(s, _):
        place = s * n
        for j in range(n):
            place = jnp.where(dest[s * n + j] // n == group, s * n + j, place)
        table[3, s] = lens[place]
        table[4, s] = rest[place]
        return 0

    lax.fori_loop(0, n, note, 0)
    for d in range(n):
        for c in fetch(d):
            c.wait()
        for c in store(d):
            c.start()
    for d in range(n):
        for c in store(d):
            c.wait()


def order_cache(dest, lens, rest, keys, values, part):
    n, length, width = keys.shape
    sm = pl.BlockSpec(memory_space=pltpu.SMEM)
    hbm = pl.BlockSpec(memory_space=pl.ANY)
    return pl.pallas_call(
        order_kernel,
        out_shape=(
            jax.ShapeDtypeStruct((n, part + length // 2, width), keys.dtype),
            jax.ShapeDtypeStruct((n, length - part, width), keys.dtype),
            jax.ShapeDtypeStruct((6, n), jnp.int32),
        ),
        in_specs=[sm, sm, sm, hbm, hbm],
        out_specs=(hbm, hbm, sm),
        scratch_shapes=[
            pltpu.VMEM((n, length // 2, width), keys.dtype),
            pltpu.VMEM(values.shape, values.dtype),
            pltpu.SemaphoreType.DMA((5, n)),
        ],
        compiler_params=pltpu.CompilerParams(vmem_limit_bytes=60 * 1024 * 1024),
        cost_estimate=pl.CostEstimate(
            flops=0, bytes_accessed=8 * keys.size, transcendentals=0
        ),
        name="order_cache",
    )(dest, lens, rest, keys, values)


def attend_kernel(turn, table, msg, keys, values, weight, keep, near, far, att, kbuf, vbuf, wbuf, sems):
    t = table[5, 0]
    n = kbuf.shape[0]
    width = wbuf.shape[1]
    chunk = width // 5

    def fetch_weight(k):
        cut = pl.ds(k * chunk, chunk)
        return pltpu.make_async_copy(weight.at[:, cut], wbuf.at[:, cut], sems.at[2, k])


    def fetch(p):
        j = table[0, t ^ ORDER[p]]
        return (
            pltpu.make_async_copy(keys.at[j], kbuf.at[p], sems.at[0, p]),
            pltpu.make_async_copy(values.at[j], vbuf.at[p], sems.at[1, p]),
        )

    for p in range(n):
        for c in fetch(p):
            c.start()
    for k in range(5):
        fetch_weight(k).start()
    col = lax.broadcasted_iota(jnp.int32, (16, keys.shape[1]), 1)
    row8 = lax.broadcasted_iota(jnp.int32, (16, 8), 0) % 4
    col8 = lax.broadcasted_iota(jnp.int32, (16, 8), 1)
    rowd = lax.broadcasted_iota(jnp.int32, (16, 128), 0) % 4
    scale = 128 ** (-0.5)
    nt = (((1,), (1,)), ((), ()))
    batch = 8
    for start in range(0, n, batch):
        ps = range(start, start + batch)
        for p in ps:
            for cp in fetch(p):
                cp.wait()
        cs = [t ^ ORDER[p] for p in ps]
        qs = [msg[c, 0:16, :] for c in cs]
        nks = [msg[c, 16:24, :] for c in cs]
        nvs = [msg[c, 24:32, :] for c in cs]
        s1 = [lax.dot_general(q, kbuf[p], nt, preferred_element_type=f32) for q, p in zip(qs, ps)]
        s2 = [lax.dot_general(q, k, nt, preferred_element_type=f32) for q, k in zip(qs, nks)]
        s1 = [jnp.where(col < table[1, c], s * scale, neg_fill) for s, c in zip(s1, cs)]
        s2 = [jnp.where(col8 <= row8, s * scale, neg_fill) for s in s2]
        m1 = [jnp.max(s, axis=1, keepdims=True) for s in s1]
        m2 = [jnp.max(s, axis=1, keepdims=True) for s in s2]
        p1 = [jnp.exp(s - m) for s, m in zip(s1, m1)]
        p2 = [jnp.exp(s - m) for s, m in zip(s2, m2)]
        o1 = [
            jnp.dot(w.astype(bf16), vbuf[p], preferred_element_type=f32) for w, p in zip(p1, ps)
        ]
        o2 = [
            jnp.dot(w.astype(bf16), v, preferred_element_type=f32) for w, v in zip(p2, nvs)
        ]
        l1 = [jnp.sum(w, axis=1, keepdims=True) for w in p1]
        l2 = [jnp.sum(w, axis=1, keepdims=True) for w in p2]
        for i, p in enumerate(ps):
            top = jnp.maximum(m1[i], m2[i])
            e1 = jnp.exp(m1[i] - top)
            e2 = jnp.exp(m2[i] - top)
            o = (e1 * o1[i] + e2 * o2[i]) / (e1 * l1[i] + e2 * l2[i])
            o = jnp.where(rowd < table[2, cs[i]], o, 0.0)
            for h in range(4):
                att[4 * p : 4 * p + 4, 128 * h : 128 * h + 128] = o[4 * h : 4 * h + 4, :]
    a = att[...].astype(bf16)
    rows = a.shape[0]
    step = 512
    for k in range(0, width, step):
        if k % chunk == 0:
            fetch_weight(k // chunk).wait()
        y = jnp.dot(a, wbuf[:, k : k + step], preferred_element_type=f32)
        keep[:, k : k + step] = y[: rows // 2]
        near[:, k : k + step] = y[rows // 2 : rows * 7 // 8].astype(bf16)
        far[:, k : k + step] = y[rows * 7 // 8 :].astype(bf16)


def attend(turn, table, msg, keys, values, weight):
    n = msg.shape[0]
    depth, out_width = weight.shape
    vm = pl.BlockSpec(memory_space=pltpu.VMEM)
    sm = pl.BlockSpec(memory_space=pltpu.SMEM)
    hbm = pl.BlockSpec(memory_space=pl.ANY)
    return pl.pallas_call(
        attend_kernel,
        out_shape=(
            jax.ShapeDtypeStruct((2 * n, out_width), f32),
            jax.ShapeDtypeStruct((n * 3 // 2, out_width), bf16),
            jax.ShapeDtypeStruct((n // 2, out_width), bf16),
        ),
        in_specs=[sm, sm, vm, hbm, hbm, hbm],
        out_specs=(vm, vm, vm),
        scratch_shapes=[
            pltpu.VMEM((4 * n, depth), f32),
            pltpu.VMEM(keys.shape, bf16),
            pltpu.VMEM(values.shape, bf16),
            pltpu.VMEM((depth, out_width), bf16),
            pltpu.SemaphoreType.DMA((3, n)),
        ],
        compiler_params=pltpu.CompilerParams(vmem_limit_bytes=48 * 1024 * 1024),
        cost_estimate=pl.CostEstimate(
            flops=4 * n * 16 * 512 * 128 + 2 * 4 * n * depth * out_width,
            bytes_accessed=4 * keys.size + 2 * weight.size,
            transcendentals=0,
        ),
        name="attend",
    )(turn, table, msg, keys, values, weight)


def place_kernel(bases, table, fresh, *refs):
    *got, out, rows = refs
    count, total, _ = out.shape

    @pl.when(pl.program_id(0) == 0)
    def _():
        rows[...] = fresh[...].astype(f32)

    slots = [pl.program_id(0) * count + b for b in range(count)]
    lengths = [table[3, s] for s in slots]
    rests = [table[4, s] for s in slots]
    helds = [jnp.where(r > 0, l, 0) for l, r in zip(lengths, rests)]
    step = 32
    for b in range(count):
        for piece, (even, odd) in zip(got, bases):
            base = even
            if odd != even:
                base = pl.multiple_of(even + table[5, 1] * (odd - even), 16)
            for k in range(0, piece.shape[1], step):
                size = min(step, piece.shape[1] - k)
                block = piece[b, k : k + size, :]
                out[b, pl.ds(base + k, size), :] = jnp.where(
                    base + k < helds[b], block, jnp.zeros((), block.dtype)
                )
    starts = [pl.multiple_of(jnp.minimum(l // 16 * 16, total - 32), 16) for l in lengths]
    windows = [out[b, pl.ds(start, 32), :].astype(f32) for b, start in enumerate(starts)]
    news = [[rows[u, pl.ds(s, 1), :] for u in range(fresh.shape[0])] for s in slots]
    place_in = lax.broadcasted_iota(jnp.int32, windows[0].shape, 0)
    for b in range(count):
        inner = place_in + starts[b]
        window = jnp.where(inner < helds[b], windows[b], 0.0)
        for u, row in enumerate(news[b]):
            spot = jnp.where(rests[b] > u, lengths[b] + u, -1)
            window = jnp.where(inner == spot, row, window)
        windows[b] = window.astype(bf16)
    for b, start in enumerate(starts):
        out[b, pl.ds(start, 32), :] = windows[b]


def place(table, fresh, *pieces):
    n, _, width = pieces[0][0].shape
    length = sum(rows for _, _, rows, _ in pieces)
    count = 8
    return pl.pallas_call(
        functools.partial(place_kernel, tuple(bases for _, _, _, bases in pieces)),
        out_shape=jax.ShapeDtypeStruct((n, length, width), bf16),
        grid=(n // count,),
        in_specs=[
            pl.BlockSpec(memory_space=pltpu.SMEM),
            pl.BlockSpec(fresh.shape, lambda i: (0, 0, 0)),
        ]
        + [
            pl.BlockSpec((count, rows, width), functools.partial(lambda k, i: (i, k, 0), start // rows))
            for _, start, rows, _ in pieces
        ],
        out_specs=pl.BlockSpec((count, length, width), lambda i: (i, 0, 0)),
        scratch_shapes=[pltpu.VMEM(fresh.shape, f32)],
        compiler_params=pltpu.CompilerParams(vmem_limit_bytes=62 * 1024 * 1024),
        cost_estimate=pl.CostEstimate(
            flops=0, bytes_accessed=4 * n * length * width, transcendentals=0
        ),
        name="place",
    )(table, fresh, *[array for array, _, _, _ in pieces])


def finish_kernel(table, *refs):
    *pieces, residual, gain, out, normed, sums = refs
    t = table[5, 0]
    rows = residual.shape[0]
    row = lax.broadcasted_iota(jnp.int32, (rows, rows), 0)
    col = lax.broadcasted_iota(jnp.int32, (rows, rows), 1)
    i = col // 4
    turned = (i & 1) * 8 + (i // 2 & 1) * 4 + (i // 4 & 1) * 2 + (i // 8 & 1)
    target = (col % 4) * 16 + (t ^ turned)
    pick = jnp.where(row == target, 1.0, 0.0).astype(bf16)
    step = 512
    total = jnp.zeros((rows, 128), f32)
    for k in range(0, residual.shape[1], step):
        cut = slice(k, k + step)
        piece = jnp.concatenate([x[:, cut].astype(f32) for x in pieces], axis=0).astype(bf16)
        level = residual[:, cut].astype(f32) + jnp.dot(pick, piece, preferred_element_type=f32)
        out[:, cut] = level.astype(bf16)
        sums[:, cut] = level
        sq = level * level
        for j in range(0, step, 128):
            total = total + sq[:, j : j + 128]
    mean = jnp.sum(total, axis=1, keepdims=True) / residual.shape[1]
    factor = lax.rsqrt(mean + eps)
    for k in range(0, residual.shape[1], step):
        cut = slice(k, k + step)
        normed[:, cut] = (sums[:, cut] * factor * gain[:, cut].astype(f32)).astype(bf16)


def finish(table, pieces, residual, gain):
    rows, width = residual.shape
    vm = pl.BlockSpec(memory_space=pltpu.VMEM)
    return pl.pallas_call(
        finish_kernel,
        out_shape=(jax.ShapeDtypeStruct((rows, width), bf16),) * 2,
        in_specs=[pl.BlockSpec(memory_space=pltpu.SMEM)] + [vm] * (len(pieces) + 2),
        out_specs=(vm, vm),
        scratch_shapes=[pltpu.VMEM((rows, width), f32)],
        compiler_params=pltpu.CompilerParams(vmem_limit_bytes=16 * 1024 * 1024),
        cost_estimate=pl.CostEstimate(
            flops=2 * rows * rows * width, bytes_accessed=8 * rows * width, transcendentals=0
        ),
        name="finish",
    )(table, *pieces, residual, gain)


def swap(x, mask):
    return lax.ppermute(x, "tensor", [(t, fold(fold(t) ^ mask)) for t in range(16)])


def hand_over(x, mask):
    return lax.ppermute(
        x,
        ("group", "tensor"),
        [
            (g * 16 + t, (g ^ fold(t)) * 16 + fold(fold(t) ^ mask))
            for g in range(16)
            for t in range(16)
        ],
    )


def on_device(
    queries,
    new_keys,
    new_values,
    key_cache,
    value_cache,
    cache_len,
    remaining,
    dest_table,
    residual_in,
    out_weight,
    norm_gain,
):
    steps, n, heads, width = queries.shape
    out_width = out_weight.shape[1]
    fresh_keys = new_keys[:, :, 0, :]
    fresh_values = new_values[:, :, 0, :]
    msg = ask(queries, fresh_keys, fresh_values)
    msg = lax.all_to_all(msg, "group", split_axis=0, concat_axis=0, tiled=True)
    old_keys, old_values = key_cache[:, 0], value_cache[:, 0]
    length = old_keys.shape[1]
    part, share = 224, length // 2
    large, small, table = order_cache(
        dest_table, cache_len, remaining, old_keys, old_values, part
    )
    large = lax.all_to_all(large, "group", split_axis=0, concat_axis=0, tiled=True)

    def first_steps(turn):
        keep, near, far = attend(turn[None], table, msg, old_keys, old_values, out_weight)
        far, near = swap(far, 1), swap(near, 1).astype(f32)
        far = swap((keep[24:] + far.astype(f32)).astype(bf16), 2)
        mid = swap((keep[16:24] + near[16:]).astype(bf16), 2)
        far = swap((keep[8:16] + near[8:16] + far.astype(f32)).astype(bf16), 4)
        s = keep[:8] + near[:8] + mid.astype(f32) + far.astype(f32)
        return s[:4], s[4:].astype(bf16)

    def no_steps(turn):
        return jnp.zeros((4, out_width), f32), jnp.zeros((4, out_width), bf16)

    tensor = lax.axis_index("tensor")
    s, send = lax.cond(tensor >= 0, first_steps, no_steps, tensor)
    s, send, large = lax.optimization_barrier((s, send, large))
    key_share = large[:, part:]
    key_other = swap(key_share, 1)

    def next_steps(s, send):
        s = (s + swap(send, 8).astype(f32)).astype(bf16)
        return jnp.concatenate([hand_over(s, m) for m in (0, 8)], axis=0)

    first = lax.cond(
        tensor >= 0,
        next_steps,
        lambda s, send: jnp.zeros((8, out_width), bf16),
        s,
        send,
    )
    first, small = lax.optimization_barrier((first, small))
    by4 = swap(first, 4)
    by2 = swap(first, 2)
    by1 = swap(first, 1)
    small = lax.all_to_all(small, "group", split_axis=0, concat_axis=0, tiled=True)
    key_out = place(
        table,
        fresh_keys,
        (key_share, 0, share, (0, share)),
        (key_other, 0, share, (share, 0)),
    )
    by4, key_out = lax.optimization_barrier((by4, key_out))
    by42 = swap(by4, 2)
    later = swap(jnp.concatenate([by4, by2], axis=0), 1)
    by42, by1 = lax.optimization_barrier((by42, by1))
    last = swap(by42, 1)
    value_out = place(
        table,
        fresh_values,
        (large, 0, part, (0, 0)),
        (small, 0, length - part, (part, part)),
    )
    last, value_out = lax.optimization_barrier((last, value_out))
    residual_out, normed = finish(
        table,
        (first, by4, by2, by42, by1, later, last),
        residual_in.reshape(steps * n, out_width),
        norm_gain.reshape(1, out_width),
    )
    return (
        residual_out.reshape(steps, n, out_width),
        normed.reshape(steps, n, out_width),
        key_out[:, None],
        value_out[:, None],
    )


def solution(mesh):
    placed = (
        P(None, "group", "tensor", None),
        P(None, "group", "tensor", None),
        P(None, "group", "tensor", None),
        P("group", "tensor", None, None),
        P("group", "tensor", None, None),
        P(),
        P(),
        P(),
        P(None, "group", None),
        P("tensor", None),
        P(),
    )
    return jax.shard_map(
        on_device,
        mesh=mesh,
        in_specs=placed,
        out_specs=(
            P(None, "group", None),
            P(None, "group", None),
            P("group", "tensor", None, None),
            P("group", "tensor", None, None),
        ),
        check_vma=False,
    )
```

```python
import functools

import jax
import jax.numpy as jnp
from jax import lax
from jax.experimental import pallas as pl
from jax.experimental.pallas import tpu as pltpu
from jax.sharding import PartitionSpec as P

neg_fill = -1e30
eps = 1e-06
ORDER = (0, 8, 4, 12, 2, 10, 6, 14, 1, 9, 5, 13, 3, 11, 7, 15)
f32 = jnp.float32
bf16 = jnp.bfloat16


def ask_kernel(queries, new_keys, new_values, msg, asked, built):
    steps, n, heads, width = queries.shape
    rows = msg.shape[1]
    asked[...] = queries[...].astype(f32).reshape(asked.shape)
    built[...] = jnp.zeros(built.shape, f32)
    for t in range(steps):
        for h in range(heads):
            built[pl.ds(4 * h + t, n, stride=rows), :] = asked[
                pl.ds(t * n * heads + h, n, stride=heads), :
            ]
        built[pl.ds(16 + t, n, stride=rows), :] = new_keys[t].astype(f32)
        built[pl.ds(24 + t, n, stride=rows), :] = new_values[t].astype(f32)
    msg[...] = built[...].astype(bf16).reshape(msg.shape)


def ask(queries, new_keys, new_values):
    steps, n, heads, width = queries.shape
    vm = pl.BlockSpec(memory_space=pltpu.VMEM)
    return pl.pallas_call(
        ask_kernel,
        out_shape=jax.ShapeDtypeStruct((n, 32, width), bf16),
        in_specs=[vm] * 3,
        out_specs=vm,
        scratch_shapes=[
            pltpu.VMEM((steps * n * heads, width), f32),
            pltpu.VMEM((n * 32, width), f32),
        ],
        compiler_params=pltpu.CompilerParams(vmem_limit_bytes=60 * 1024 * 1024),
        cost_estimate=pl.CostEstimate(flops=0, bytes_accessed=400000, transcendentals=0),
        name="ask",
    )(queries, new_keys, new_values)


def fold(t):
    return t ^ (3 * (t // 4 % 2))


def order_kernel(dest, lens, rest, keys, values, large, small, table, kbuf, vbuf, sems):
    n, length, _ = keys.shape
    part = length - small.shape[1]
    share = large.shape[1] - part
    group = lax.axis_index("group")
    tensor = lax.axis_index("tensor")
    table[5, 0] = fold(tensor) ^ group
    table[5, 1] = tensor & 1
    base = pl.multiple_of((tensor & 1) * share, 16)
    for j in range(n):
        d = dest[group * n + j] // n
        table[0, d] = j
        table[1, d] = lens[group * n + j]
        table[2, d] = rest[group * n + j]

    def fetch(d):
        j = table[0, d]
        return (
            pltpu.make_async_copy(
                keys.at[j, pl.ds(base, share)], kbuf.at[d], sems.at[0, d]
            ),
            pltpu.make_async_copy(values.at[j], vbuf.at[d], sems.at[1, d]),
        )

    def store(d):
        return (
            pltpu.make_async_copy(kbuf.at[d], large.at[d, pl.ds(part, share)], sems.at[2, d]),
            pltpu.make_async_copy(
                vbuf.at[d, pl.ds(0, part)], large.at[d, pl.ds(0, part)], sems.at[3, d]
            ),
            pltpu.make_async_copy(
                vbuf.at[d, pl.ds(part, length - part)], small.at[d], sems.at[4, d]
            ),
        )

    for d in range(n):
        for c in fetch(d):
            c.start()

    def note(s, _):
        place = s * n
        for j in range(n):
            place = jnp.where(dest[s * n + j] // n == group, s * n + j, place)
        table[3, s] = lens[place]
        table[4, s] = rest[place]
        return 0

    lax.fori_loop(0, n, note, 0)
    for d in range(n):
        for c in fetch(d):
            c.wait()
        for c in store(d):
            c.start()
    for d in range(n):
        for c in store(d):
            c.wait()


def order_cache(dest, lens, rest, keys, values, part):
    n, length, width = keys.shape
    sm = pl.BlockSpec(memory_space=pltpu.SMEM)
    hbm = pl.BlockSpec(memory_space=pl.ANY)
    return pl.pallas_call(
        order_kernel,
        out_shape=(
            jax.ShapeDtypeStruct((n, part + length // 2, width), keys.dtype),
            jax.ShapeDtypeStruct((n, length - part, width), keys.dtype),
            jax.ShapeDtypeStruct((6, n), jnp.int32),
        ),
        in_specs=[sm, sm, sm, hbm, hbm],
        out_specs=(hbm, hbm, sm),
        scratch_shapes=[
            pltpu.VMEM((n, length // 2, width), keys.dtype),
            pltpu.VMEM(values.shape, values.dtype),
            pltpu.SemaphoreType.DMA((5, n)),
        ],
        compiler_params=pltpu.CompilerParams(vmem_limit_bytes=60 * 1024 * 1024),
        cost_estimate=pl.CostEstimate(
            flops=0, bytes_accessed=8 * keys.size, transcendentals=0
        ),
        name="order_cache",
    )(dest, lens, rest, keys, values)


def attend_kernel(turn, table, msg, keys, values, weight, keep, near, far, att, kbuf, vbuf, wbuf, sems):
    t = table[5, 0]
    n = kbuf.shape[0]
    width = wbuf.shape[1]
    chunk = width // 5

    def fetch_weight(k):
        cut = pl.ds(k * chunk, chunk)
        return pltpu.make_async_copy(weight.at[:, cut], wbuf.at[:, cut], sems.at[2, k])


    def fetch(p):
        j = table[0, t ^ ORDER[p]]
        return (
            pltpu.make_async_copy(keys.at[j], kbuf.at[p], sems.at[0, p]),
            pltpu.make_async_copy(values.at[j], vbuf.at[p], sems.at[1, p]),
        )

    for p in range(n):
        for c in fetch(p):
            c.start()
    for k in range(5):
        fetch_weight(k).start()
    col = lax.broadcasted_iota(jnp.int32, (16, keys.shape[1]), 1)
    row8 = lax.broadcasted_iota(jnp.int32, (16, 8), 0) % 4
    col8 = lax.broadcasted_iota(jnp.int32, (16, 8), 1)
    rowd = lax.broadcasted_iota(jnp.int32, (16, 128), 0) % 4
    scale = 128 ** (-0.5)
    nt = (((1,), (1,)), ((), ()))
    batch = 8
    for start in range(0, n, batch):
        ps = range(start, start + batch)
        for p in ps:
            for cp in fetch(p):
                cp.wait()
        cs = [t ^ ORDER[p] for p in ps]
        qs = [msg[c, 0:16, :] for c in cs]
        nks = [msg[c, 16:24, :] for c in cs]
        nvs = [msg[c, 24:32, :] for c in cs]
        s1 = [lax.dot_general(q, kbuf[p], nt, preferred_element_type=f32) for q, p in zip(qs, ps)]
        s2 = [lax.dot_general(q, k, nt, preferred_element_type=f32) for q, k in zip(qs, nks)]
        s1 = [jnp.where(col < table[1, c], s * scale, neg_fill) for s, c in zip(s1, cs)]
        s2 = [jnp.where(col8 <= row8, s * scale, neg_fill) for s in s2]
        m1 = [jnp.max(s, axis=1, keepdims=True) for s in s1]
        m2 = [jnp.max(s, axis=1, keepdims=True) for s in s2]
        p1 = [jnp.exp(s - m) for s, m in zip(s1, m1)]
        p2 = [jnp.exp(s - m) for s, m in zip(s2, m2)]
        o1 = [
            jnp.dot(w.astype(bf16), vbuf[p], preferred_element_type=f32) for w, p in zip(p1, ps)
        ]
        o2 = [
            jnp.dot(w.astype(bf16), v, preferred_element_type=f32) for w, v in zip(p2, nvs)
        ]
        l1 = [jnp.sum(w, axis=1, keepdims=True) for w in p1]
        l2 = [jnp.sum(w, axis=1, keepdims=True) for w in p2]
        for i, p in enumerate(ps):
            top = jnp.maximum(m1[i], m2[i])
            e1 = jnp.exp(m1[i] - top)
            e2 = jnp.exp(m2[i] - top)
            o = (e1 * o1[i] + e2 * o2[i]) / (e1 * l1[i] + e2 * l2[i])
            o = jnp.where(rowd < table[2, cs[i]], o, 0.0)
            for h in range(4):
                att[4 * p : 4 * p + 4, 128 * h : 128 * h + 128] = o[4 * h : 4 * h + 4, :]
    a = att[...].astype(bf16)
    rows = a.shape[0]
    step = 512
    for k in range(0, width, step):
        if k % chunk == 0:
            fetch_weight(k // chunk).wait()
        y = jnp.dot(a, wbuf[:, k : k + step], preferred_element_type=f32)
        keep[:, k : k + step] = y[: rows // 2]
        near[:, k : k + step] = y[rows // 2 : rows * 7 // 8].astype(bf16)
        far[:, k : k + step] = y[rows * 7 // 8 :].astype(bf16)


def attend(turn, table, msg, keys, values, weight):
    n = msg.shape[0]
    depth, out_width = weight.shape
    vm = pl.BlockSpec(memory_space=pltpu.VMEM)
    sm = pl.BlockSpec(memory_space=pltpu.SMEM)
    hbm = pl.BlockSpec(memory_space=pl.ANY)
    return pl.pallas_call(
        attend_kernel,
        out_shape=(
            jax.ShapeDtypeStruct((2 * n, out_width), f32),
            jax.ShapeDtypeStruct((n * 3 // 2, out_width), bf16),
            jax.ShapeDtypeStruct((n // 2, out_width), bf16),
        ),
        in_specs=[sm, sm, vm, hbm, hbm, hbm],
        out_specs=(vm, vm, vm),
        scratch_shapes=[
            pltpu.VMEM((4 * n, depth), f32),
            pltpu.VMEM(keys.shape, bf16),
            pltpu.VMEM(values.shape, bf16),
            pltpu.VMEM((depth, out_width), bf16),
            pltpu.SemaphoreType.DMA((3, n)),
        ],
        compiler_params=pltpu.CompilerParams(vmem_limit_bytes=48 * 1024 * 1024),
        cost_estimate=pl.CostEstimate(
            flops=4 * n * 16 * 512 * 128 + 2 * 4 * n * depth * out_width,
            bytes_accessed=4 * keys.size + 2 * weight.size,
            transcendentals=0,
        ),
        name="attend",
    )(turn, table, msg, keys, values, weight)


def place_kernel(bases, table, fresh, *refs):
    *got, out, rows = refs
    count, total, _ = out.shape

    @pl.when(pl.program_id(0) == 0)
    def _():
        rows[...] = fresh[...].astype(f32)

    slots = [pl.program_id(0) * count + b for b in range(count)]
    lengths = [table[3, s] for s in slots]
    rests = [table[4, s] for s in slots]
    helds = [jnp.where(r > 0, l, 0) for l, r in zip(lengths, rests)]
    step = 32
    for b in range(count):
        for piece, (even, odd) in zip(got, bases):
            base = even
            if odd != even:
                base = pl.multiple_of(even + table[5, 1] * (odd - even), 16)
            for k in range(0, piece.shape[1], step):
                size = min(step, piece.shape[1] - k)
                block = piece[b, k : k + size, :]
                out[b, pl.ds(base + k, size), :] = jnp.where(
                    base + k < helds[b], block, jnp.zeros((), block.dtype)
                )
    starts = [pl.multiple_of(jnp.minimum(l // 16 * 16, total - 32), 16) for l in lengths]
    windows = [out[b, pl.ds(start, 32), :].astype(f32) for b, start in enumerate(starts)]
    news = [[rows[u, pl.ds(s, 1), :] for u in range(fresh.shape[0])] for s in slots]
    place_in = lax.broadcasted_iota(jnp.int32, windows[0].shape, 0)
    for b in range(count):
        inner = place_in + starts[b]
        window = jnp.where(inner < helds[b], windows[b], 0.0)
        for u, row in enumerate(news[b]):
            spot = jnp.where(rests[b] > u, lengths[b] + u, -1)
            window = jnp.where(inner == spot, row, window)
        windows[b] = window.astype(bf16)
    for b, start in enumerate(starts):
        out[b, pl.ds(start, 32), :] = windows[b]


def place(table, fresh, *pieces):
    n, _, width = pieces[0][0].shape
    length = sum(rows for _, _, rows, _ in pieces)
    count = 8
    return pl.pallas_call(
        functools.partial(place_kernel, tuple(bases for _, _, _, bases in pieces)),
        out_shape=jax.ShapeDtypeStruct((n, length, width), bf16),
        grid=(n // count,),
        in_specs=[
            pl.BlockSpec(memory_space=pltpu.SMEM),
            pl.BlockSpec(fresh.shape, lambda i: (0, 0, 0)),
        ]
        + [
            pl.BlockSpec((count, rows, width), functools.partial(lambda k, i: (i, k, 0), start // rows))
            for _, start, rows, _ in pieces
        ],
        out_specs=pl.BlockSpec((count, length, width), lambda i: (i, 0, 0)),
        scratch_shapes=[pltpu.VMEM(fresh.shape, f32)],
        compiler_params=pltpu.CompilerParams(vmem_limit_bytes=62 * 1024 * 1024),
        cost_estimate=pl.CostEstimate(
            flops=0, bytes_accessed=4 * n * length * width, transcendentals=0
        ),
        name="place",
    )(table, fresh, *[array for array, _, _, _ in pieces])


def finish_kernel(table, *refs):
    *pieces, residual, gain, out, normed, sums = refs
    t = table[5, 0]
    rows = residual.shape[0]
    row = lax.broadcasted_iota(jnp.int32, (rows, rows), 0)
    col = lax.broadcasted_iota(jnp.int32, (rows, rows), 1)
    i = col // 4
    turned = (i & 1) * 8 + (i // 2 & 1) * 4 + (i // 4 & 1) * 2 + (i // 8 & 1)
    target = (col % 4) * 16 + (t ^ turned)
    pick = jnp.where(row == target, 1.0, 0.0).astype(bf16)
    step = 512
    total = jnp.zeros((rows, 128), f32)
    for k in range(0, residual.shape[1], step):
        cut = slice(k, k + step)
        piece = jnp.concatenate([x[:, cut].astype(f32) for x in pieces], axis=0).astype(bf16)
        level = residual[:, cut].astype(f32) + jnp.dot(pick, piece, preferred_element_type=f32)
        out[:, cut] = level.astype(bf16)
        sums[:, cut] = level
        sq = level * level
        for j in range(0, step, 128):
            total = total + sq[:, j : j + 128]
    mean = jnp.sum(total, axis=1, keepdims=True) / residual.shape[1]
    factor = lax.rsqrt(mean + eps)
    for k in range(0, residual.shape[1], step):
        cut = slice(k, k + step)
        normed[:, cut] = (sums[:, cut] * factor * gain[:, cut].astype(f32)).astype(bf16)


def finish(table, pieces, residual, gain):
    rows, width = residual.shape
    vm = pl.BlockSpec(memory_space=pltpu.VMEM)
    return pl.pallas_call(
        finish_kernel,
        out_shape=(jax.ShapeDtypeStruct((rows, width), bf16),) * 2,
        in_specs=[pl.BlockSpec(memory_space=pltpu.SMEM)] + [vm] * (len(pieces) + 2),
        out_specs=(vm, vm),
        scratch_shapes=[pltpu.VMEM((rows, width), f32)],
        compiler_params=pltpu.CompilerParams(vmem_limit_bytes=16 * 1024 * 1024),
        cost_estimate=pl.CostEstimate(
            flops=2 * rows * rows * width, bytes_accessed=8 * rows * width, transcendentals=0
        ),
        name="finish",
    )(table, *pieces, residual, gain)


def swap(x, mask):
    return lax.ppermute(x, "tensor", [(t, fold(fold(t) ^ mask)) for t in range(16)])


def hand_over(x, mask):
    return lax.ppermute(
        x,
        ("group", "tensor"),
        [
            (g * 16 + t, (g ^ fold(t)) * 16 + fold(fold(t) ^ mask))
            for g in range(16)
            for t in range(16)
        ],
    )


def on_device(
    queries,
    new_keys,
    new_values,
    key_cache,
    value_cache,
    cache_len,
    remaining,
    dest_table,
    residual_in,
    out_weight,
    norm_gain,
):
    steps, n, heads, width = queries.shape
    out_width = out_weight.shape[1]
    fresh_keys = new_keys[:, :, 0, :]
    fresh_values = new_values[:, :, 0, :]
    msg = ask(queries, fresh_keys, fresh_values)
    msg = lax.all_to_all(msg, "group", split_axis=0, concat_axis=0, tiled=True)
    old_keys, old_values = key_cache[:, 0], value_cache[:, 0]
    length = old_keys.shape[1]
    part, share = 224, length // 2
    large, small, table = order_cache(
        dest_table, cache_len, remaining, old_keys, old_values, part
    )
    large = lax.all_to_all(large, "group", split_axis=0, concat_axis=0, tiled=True)

    def first_steps(turn):
        keep, near, far = attend(turn[None], table, msg, old_keys, old_values, out_weight)
        far, near = swap(far, 1), swap(near, 1).astype(f32)
        far = swap((keep[24:] + far.astype(f32)).astype(bf16), 2)
        mid = swap((keep[16:24] + near[16:]).astype(bf16), 2)
        far = swap((keep[8:16] + near[8:16] + far.astype(f32)).astype(bf16), 4)
        s = keep[:8] + near[:8] + mid.astype(f32) + far.astype(f32)
        return s[:4], s[4:].astype(bf16)

    def no_steps(turn):
        return jnp.zeros((4, out_width), f32), jnp.zeros((4, out_width), bf16)

    tensor = lax.axis_index("tensor")
    s, send = lax.cond(tensor >= 0, first_steps, no_steps, tensor)
    s, send, large = lax.optimization_barrier((s, send, large))
    key_share = large[:, part:]
    key_other = swap(key_share, 1)

    def next_steps(s, send):
        s = (s + swap(send, 8).astype(f32)).astype(bf16)
        return jnp.concatenate([hand_over(s, m) for m in (0, 8)], axis=0)

    first = lax.cond(
        tensor >= 0,
        next_steps,
        lambda s, send: jnp.zeros((8, out_width), bf16),
        s,
        send,
    )
    first, small = lax.optimization_barrier((first, small))
    by4 = swap(first, 4)
    by2 = swap(first, 2)
    by1 = swap(first, 1)
    small = lax.all_to_all(small, "group", split_axis=0, concat_axis=0, tiled=True)
    key_out = place(
        table,
        fresh_keys,
        (key_share, 0, share, (0, share)),
        (key_other, 0, share, (share, 0)),
    )
    by42 = swap(by4, 2)
    later = swap(jnp.concatenate([by4, by2], axis=0), 1)
    by42, by1, key_out = lax.optimization_barrier((by42, by1, key_out))
    last = swap(by42, 1)
    value_out = place(
        table,
        fresh_values,
        (large, 0, part, (0, 0)),
        (small, 0, length - part, (part, part)),
    )
    last, value_out = lax.optimization_barrier((last, value_out))
    residual_out, normed = finish(
        table,
        (first, by4, by2, by42, by1, later, last),
        residual_in.reshape(steps * n, out_width),
        norm_gain.reshape(1, out_width),
    )
    return (
        residual_out.reshape(steps, n, out_width),
        normed.reshape(steps, n, out_width),
        key_out[:, None],
        value_out[:, None],
    )


def solution(mesh):
    placed = (
        P(None, "group", "tensor", None),
        P(None, "group", "tensor", None),
        P(None, "group", "tensor", None),
        P("group", "tensor", None, None),
        P("group", "tensor", None, None),
        P(),
        P(),
        P(),
        P(None, "group", None),
        P("tensor", None),
        P(),
    )
    return jax.shard_map(
        on_device,
        mesh=mesh,
        in_specs=placed,
        out_specs=(
            P(None, "group", None),
            P(None, "group", None),
            P("group", "tensor", None, None),
            P("group", "tensor", None, None),
        ),
        check_vma=False,
    )
```

```python
import functools

import jax
import jax.numpy as jnp
from jax import lax
from jax.experimental import pallas as pl
from jax.experimental.pallas import tpu as pltpu
from jax.sharding import PartitionSpec as P

neg_fill = -1e30
eps = 1e-06
ORDER = (0, 8, 4, 12, 2, 10, 6, 14, 1, 9, 5, 13, 3, 11, 7, 15)
f32 = jnp.float32
bf16 = jnp.bfloat16


def ask_kernel(queries, new_keys, new_values, msg, asked, built):
    steps, n, heads, width = queries.shape
    rows = msg.shape[1]
    asked[...] = queries[...].astype(f32).reshape(asked.shape)
    built[...] = jnp.zeros(built.shape, f32)
    for t in range(steps):
        for h in range(heads):
            built[pl.ds(4 * h + t, n, stride=rows), :] = asked[
                pl.ds(t * n * heads + h, n, stride=heads), :
            ]
        built[pl.ds(16 + t, n, stride=rows), :] = new_keys[t].astype(f32)
        built[pl.ds(24 + t, n, stride=rows), :] = new_values[t].astype(f32)
    msg[...] = built[...].astype(bf16).reshape(msg.shape)


def ask(queries, new_keys, new_values):
    steps, n, heads, width = queries.shape
    vm = pl.BlockSpec(memory_space=pltpu.VMEM)
    return pl.pallas_call(
        ask_kernel,
        out_shape=jax.ShapeDtypeStruct((n, 32, width), bf16),
        in_specs=[vm] * 3,
        out_specs=vm,
        scratch_shapes=[
            pltpu.VMEM((steps * n * heads, width), f32),
            pltpu.VMEM((n * 32, width), f32),
        ],
        compiler_params=pltpu.CompilerParams(vmem_limit_bytes=60 * 1024 * 1024),
        cost_estimate=pl.CostEstimate(flops=0, bytes_accessed=400000, transcendentals=0),
        name="ask",
    )(queries, new_keys, new_values)


def fold(t):
    return t ^ (3 * (t // 4 % 2))


def order_kernel(dest, lens, rest, keys, values, large, small, table, kbuf, vbuf, sems):
    n, length, _ = keys.shape
    part = length - small.shape[1]
    share = large.shape[1] - part
    group = lax.axis_index("group")
    tensor = lax.axis_index("tensor")
    table[5, 0] = fold(tensor) ^ group
    table[5, 1] = tensor & 1
    base = pl.multiple_of((tensor & 1) * share, 16)
    for j in range(n):
        d = dest[group * n + j] // n
        table[0, d] = j
        table[1, d] = lens[group * n + j]
        table[2, d] = rest[group * n + j]

    def fetch(d):
        j = table[0, d]
        return (
            pltpu.make_async_copy(
                keys.at[j, pl.ds(base, share)], kbuf.at[d], sems.at[0, d]
            ),
            pltpu.make_async_copy(values.at[j], vbuf.at[d], sems.at[1, d]),
        )

    def store(d):
        return (
            pltpu.make_async_copy(kbuf.at[d], large.at[d, pl.ds(part, share)], sems.at[2, d]),
            pltpu.make_async_copy(
                vbuf.at[d, pl.ds(0, part)], large.at[d, pl.ds(0, part)], sems.at[3, d]
            ),
            pltpu.make_async_copy(
                vbuf.at[d, pl.ds(part, length - part)], small.at[d], sems.at[4, d]
            ),
        )

    for d in range(n):
        for c in fetch(d):
            c.start()

    def note(s, _):
        place = s * n
        for j in range(n):
            place = jnp.where(dest[s * n + j] // n == group, s * n + j, place)
        table[3, s] = lens[place]
        table[4, s] = rest[place]
        return 0

    lax.fori_loop(0, n, note, 0)
    for d in range(n):
        for c in fetch(d):
            c.wait()
        for c in store(d):
            c.start()
    for d in range(n):
        for c in store(d):
            c.wait()


def order_cache(dest, lens, rest, keys, values, part):
    n, length, width = keys.shape
    sm = pl.BlockSpec(memory_space=pltpu.SMEM)
    hbm = pl.BlockSpec(memory_space=pl.ANY)
    return pl.pallas_call(
        order_kernel,
        out_shape=(
            jax.ShapeDtypeStruct((n, part + length // 2, width), keys.dtype),
            jax.ShapeDtypeStruct((n, length - part, width), keys.dtype),
            jax.ShapeDtypeStruct((6, n), jnp.int32),
        ),
        in_specs=[sm, sm, sm, hbm, hbm],
        out_specs=(hbm, hbm, sm),
        scratch_shapes=[
            pltpu.VMEM((n, length // 2, width), keys.dtype),
            pltpu.VMEM(values.shape, values.dtype),
            pltpu.SemaphoreType.DMA((5, n)),
        ],
        compiler_params=pltpu.CompilerParams(vmem_limit_bytes=60 * 1024 * 1024),
        cost_estimate=pl.CostEstimate(
            flops=0, bytes_accessed=8 * keys.size, transcendentals=0
        ),
        name="order_cache",
    )(dest, lens, rest, keys, values)


def attend_kernel(turn, table, msg, keys, values, weight, keep, near, far, att, kbuf, vbuf, wbuf, sems):
    t = table[5, 0]
    n = kbuf.shape[0]
    width = wbuf.shape[1]
    chunk = width // 5

    def fetch_weight(k):
        cut = pl.ds(k * chunk, chunk)
        return pltpu.make_async_copy(weight.at[:, cut], wbuf.at[:, cut], sems.at[2, k])


    def fetch(p):
        j = table[0, t ^ ORDER[p]]
        return (
            pltpu.make_async_copy(keys.at[j], kbuf.at[p], sems.at[0, p]),
            pltpu.make_async_copy(values.at[j], vbuf.at[p], sems.at[1, p]),
        )

    for p in range(n):
        for c in fetch(p):
            c.start()
    for k in range(5):
        fetch_weight(k).start()
    col = lax.broadcasted_iota(jnp.int32, (16, keys.shape[1]), 1)
    row8 = lax.broadcasted_iota(jnp.int32, (16, 8), 0) % 4
    col8 = lax.broadcasted_iota(jnp.int32, (16, 8), 1)
    rowd = lax.broadcasted_iota(jnp.int32, (16, 128), 0) % 4
    scale = 128 ** (-0.5)
    nt = (((1,), (1,)), ((), ()))
    batch = 8
    for start in range(0, n, batch):
        ps = range(start, start + batch)
        for p in ps:
            for cp in fetch(p):
                cp.wait()
        cs = [t ^ ORDER[p] for p in ps]
        qs = [msg[c, 0:16, :] for c in cs]
        nks = [msg[c, 16:24, :] for c in cs]
        nvs = [msg[c, 24:32, :] for c in cs]
        s1 = [lax.dot_general(q, kbuf[p], nt, preferred_element_type=f32) for q, p in zip(qs, ps)]
        s2 = [lax.dot_general(q, k, nt, preferred_element_type=f32) for q, k in zip(qs, nks)]
        s1 = [jnp.where(col < table[1, c], s * scale, neg_fill) for s, c in zip(s1, cs)]
        s2 = [jnp.where(col8 <= row8, s * scale, neg_fill) for s in s2]
        m1 = [jnp.max(s, axis=1, keepdims=True) for s in s1]
        m2 = [jnp.max(s, axis=1, keepdims=True) for s in s2]
        p1 = [jnp.exp(s - m) for s, m in zip(s1, m1)]
        p2 = [jnp.exp(s - m) for s, m in zip(s2, m2)]
        o1 = [
            jnp.dot(w.astype(bf16), vbuf[p], preferred_element_type=f32) for w, p in zip(p1, ps)
        ]
        o2 = [
            jnp.dot(w.astype(bf16), v, preferred_element_type=f32) for w, v in zip(p2, nvs)
        ]
        l1 = [jnp.sum(w, axis=1, keepdims=True) for w in p1]
        l2 = [jnp.sum(w, axis=1, keepdims=True) for w in p2]
        for i, p in enumerate(ps):
            top = jnp.maximum(m1[i], m2[i])
            e1 = jnp.exp(m1[i] - top)
            e2 = jnp.exp(m2[i] - top)
            o = (e1 * o1[i] + e2 * o2[i]) / (e1 * l1[i] + e2 * l2[i])
            o = jnp.where(rowd < table[2, cs[i]], o, 0.0)
            for h in range(4):
                att[4 * p : 4 * p + 4, 128 * h : 128 * h + 128] = o[4 * h : 4 * h + 4, :]
    a = att[...].astype(bf16)
    rows = a.shape[0]
    step = 512
    for k in range(0, width, step):
        if k % chunk == 0:
            fetch_weight(k // chunk).wait()
        y = jnp.dot(a, wbuf[:, k : k + step], preferred_element_type=f32)
        keep[:, k : k + step] = y[: rows // 2]
        near[:, k : k + step] = y[rows // 2 : rows * 7 // 8].astype(bf16)
        far[:, k : k + step] = y[rows * 7 // 8 :].astype(bf16)


def attend(turn, table, msg, keys, values, weight):
    n = msg.shape[0]
    depth, out_width = weight.shape
    vm = pl.BlockSpec(memory_space=pltpu.VMEM)
    sm = pl.BlockSpec(memory_space=pltpu.SMEM)
    hbm = pl.BlockSpec(memory_space=pl.ANY)
    return pl.pallas_call(
        attend_kernel,
        out_shape=(
            jax.ShapeDtypeStruct((2 * n, out_width), f32),
            jax.ShapeDtypeStruct((n * 3 // 2, out_width), bf16),
            jax.ShapeDtypeStruct((n // 2, out_width), bf16),
        ),
        in_specs=[sm, sm, vm, hbm, hbm, hbm],
        out_specs=(vm, vm, vm),
        scratch_shapes=[
            pltpu.VMEM((4 * n, depth), f32),
            pltpu.VMEM(keys.shape, bf16),
            pltpu.VMEM(values.shape, bf16),
            pltpu.VMEM((depth, out_width), bf16),
            pltpu.SemaphoreType.DMA((3, n)),
        ],
        compiler_params=pltpu.CompilerParams(vmem_limit_bytes=48 * 1024 * 1024),
        cost_estimate=pl.CostEstimate(
            flops=4 * n * 16 * 512 * 128 + 2 * 4 * n * depth * out_width,
            bytes_accessed=4 * keys.size + 2 * weight.size,
            transcendentals=0,
        ),
        name="attend",
    )(turn, table, msg, keys, values, weight)


def place_kernel(bases, table, fresh, *refs):
    *got, out, rows = refs
    count, total, _ = out.shape

    @pl.when(pl.program_id(0) == 0)
    def _():
        rows[...] = fresh[...].astype(f32)

    slots = [pl.program_id(0) * count + b for b in range(count)]
    lengths = [table[3, s] for s in slots]
    rests = [table[4, s] for s in slots]
    helds = [jnp.where(r > 0, l, 0) for l, r in zip(lengths, rests)]
    step = 32
    for b in range(count):
        for piece, (even, odd) in zip(got, bases):
            base = even
            if odd != even:
                base = pl.multiple_of(even + table[5, 1] * (odd - even), 16)
            for k in range(0, piece.shape[1], step):
                size = min(step, piece.shape[1] - k)
                block = piece[b, k : k + size, :]
                out[b, pl.ds(base + k, size), :] = jnp.where(
                    base + k < helds[b], block, jnp.zeros((), block.dtype)
                )
    starts = [pl.multiple_of(jnp.minimum(l // 16 * 16, total - 32), 16) for l in lengths]
    windows = [out[b, pl.ds(start, 32), :].astype(f32) for b, start in enumerate(starts)]
    news = [[rows[u, pl.ds(s, 1), :] for u in range(fresh.shape[0])] for s in slots]
    place_in = lax.broadcasted_iota(jnp.int32, windows[0].shape, 0)
    for b in range(count):
        inner = place_in + starts[b]
        window = jnp.where(inner < helds[b], windows[b], 0.0)
        for u, row in enumerate(news[b]):
            spot = jnp.where(rests[b] > u, lengths[b] + u, -1)
            window = jnp.where(inner == spot, row, window)
        windows[b] = window.astype(bf16)
    for b, start in enumerate(starts):
        out[b, pl.ds(start, 32), :] = windows[b]


def place(table, fresh, *pieces):
    n, _, width = pieces[0][0].shape
    length = sum(rows for _, _, rows, _ in pieces)
    count = 8
    return pl.pallas_call(
        functools.partial(place_kernel, tuple(bases for _, _, _, bases in pieces)),
        out_shape=jax.ShapeDtypeStruct((n, length, width), bf16),
        grid=(n // count,),
        in_specs=[
            pl.BlockSpec(memory_space=pltpu.SMEM),
            pl.BlockSpec(fresh.shape, lambda i: (0, 0, 0)),
        ]
        + [
            pl.BlockSpec((count, rows, width), functools.partial(lambda k, i: (i, k, 0), start // rows))
            for _, start, rows, _ in pieces
        ],
        out_specs=pl.BlockSpec((count, length, width), lambda i: (i, 0, 0)),
        scratch_shapes=[pltpu.VMEM(fresh.shape, f32)],
        compiler_params=pltpu.CompilerParams(vmem_limit_bytes=62 * 1024 * 1024),
        cost_estimate=pl.CostEstimate(
            flops=0, bytes_accessed=4 * n * length * width, transcendentals=0
        ),
        name="place",
    )(table, fresh, *[array for array, _, _, _ in pieces])


def finish_kernel(table, *refs):
    *pieces, residual, gain, out, normed, sums = refs
    t = table[5, 0]
    rows = residual.shape[0]
    row = lax.broadcasted_iota(jnp.int32, (rows, rows), 0)
    col = lax.broadcasted_iota(jnp.int32, (rows, rows), 1)
    i = col // 4
    turned = (i & 1) * 8 + (i // 2 & 1) * 4 + (i // 4 & 1) * 2 + (i // 8 & 1)
    target = (col % 4) * 16 + (t ^ turned)
    pick = jnp.where(row == target, 1.0, 0.0).astype(bf16)
    step = 512
    total = jnp.zeros((rows, 128), f32)
    for k in range(0, residual.shape[1], step):
        cut = slice(k, k + step)
        piece = jnp.concatenate([x[:, cut].astype(f32) for x in pieces], axis=0).astype(bf16)
        level = residual[:, cut].astype(f32) + jnp.dot(pick, piece, preferred_element_type=f32)
        out[:, cut] = level.astype(bf16)
        sums[:, cut] = level
        sq = level * level
        for j in range(0, step, 128):
            total = total + sq[:, j : j + 128]
    mean = jnp.sum(total, axis=1, keepdims=True) / residual.shape[1]
    factor = lax.rsqrt(mean + eps)
    for k in range(0, residual.shape[1], step):
        cut = slice(k, k + step)
        normed[:, cut] = (sums[:, cut] * factor * gain[:, cut].astype(f32)).astype(bf16)


def finish(table, pieces, residual, gain):
    rows, width = residual.shape
    vm = pl.BlockSpec(memory_space=pltpu.VMEM)
    return pl.pallas_call(
        finish_kernel,
        out_shape=(jax.ShapeDtypeStruct((rows, width), bf16),) * 2,
        in_specs=[pl.BlockSpec(memory_space=pltpu.SMEM)] + [vm] * (len(pieces) + 2),
        out_specs=(vm, vm),
        scratch_shapes=[pltpu.VMEM((rows, width), f32)],
        compiler_params=pltpu.CompilerParams(vmem_limit_bytes=16 * 1024 * 1024),
        cost_estimate=pl.CostEstimate(
            flops=2 * rows * rows * width, bytes_accessed=8 * rows * width, transcendentals=0
        ),
        name="finish",
    )(table, *pieces, residual, gain)


def swap(x, mask):
    return lax.ppermute(x, "tensor", [(t, fold(fold(t) ^ mask)) for t in range(16)])


def hand_over(x, mask):
    return lax.ppermute(
        x,
        ("group", "tensor"),
        [
            (g * 16 + t, (g ^ fold(t)) * 16 + fold(fold(t) ^ mask))
            for g in range(16)
            for t in range(16)
        ],
    )


def on_device(
    queries,
    new_keys,
    new_values,
    key_cache,
    value_cache,
    cache_len,
    remaining,
    dest_table,
    residual_in,
    out_weight,
    norm_gain,
):
    steps, n, heads, width = queries.shape
    out_width = out_weight.shape[1]
    fresh_keys = new_keys[:, :, 0, :]
    fresh_values = new_values[:, :, 0, :]
    msg = ask(queries, fresh_keys, fresh_values)
    msg = lax.all_to_all(msg, "group", split_axis=0, concat_axis=0, tiled=True)
    old_keys, old_values = key_cache[:, 0], value_cache[:, 0]
    length = old_keys.shape[1]
    part, share = 208, length // 2
    large, small, table = order_cache(
        dest_table, cache_len, remaining, old_keys, old_values, part
    )
    large = lax.all_to_all(large, "group", split_axis=0, concat_axis=0, tiled=True)

    def first_steps(turn):
        keep, near, far = attend(turn[None], table, msg, old_keys, old_values, out_weight)
        far, near = swap(far, 1), swap(near, 1).astype(f32)
        far = swap((keep[24:] + far.astype(f32)).astype(bf16), 2)
        mid = swap((keep[16:24] + near[16:]).astype(bf16), 2)
        far = swap((keep[8:16] + near[8:16] + far.astype(f32)).astype(bf16), 4)
        s = keep[:8] + near[:8] + mid.astype(f32) + far.astype(f32)
        return s[:4], s[4:].astype(bf16)

    def no_steps(turn):
        return jnp.zeros((4, out_width), f32), jnp.zeros((4, out_width), bf16)

    tensor = lax.axis_index("tensor")
    s, send = lax.cond(tensor >= 0, first_steps, no_steps, tensor)
    s, send, large = lax.optimization_barrier((s, send, large))
    key_share = large[:, part:]
    key_other = swap(key_share, 1)

    def next_steps(s, send):
        s = (s + swap(send, 8).astype(f32)).astype(bf16)
        return jnp.concatenate([hand_over(s, m) for m in (0, 8)], axis=0)

    first = lax.cond(
        tensor >= 0,
        next_steps,
        lambda s, send: jnp.zeros((8, out_width), bf16),
        s,
        send,
    )
    first, small = lax.optimization_barrier((first, small))
    by4 = swap(first, 4)
    by2 = swap(first, 2)
    by1 = swap(first, 1)
    small = lax.all_to_all(small, "group", split_axis=0, concat_axis=0, tiled=True)
    key_out = place(
        table,
        fresh_keys,
        (key_share, 0, share, (0, share)),
        (key_other, 0, share, (share, 0)),
    )
    by42 = swap(by4, 2)
    later = swap(jnp.concatenate([by4, by2], axis=0), 1)
    by42, by1, key_out = lax.optimization_barrier((by42, by1, key_out))
    last = swap(by42, 1)
    value_out = place(
        table,
        fresh_values,
        (large, 0, part, (0, 0)),
        (small, 0, length - part, (part, part)),
    )
    last, value_out = lax.optimization_barrier((last, value_out))
    residual_out, normed = finish(
        table,
        (first, by4, by2, by42, by1, later, last),
        residual_in.reshape(steps * n, out_width),
        norm_gain.reshape(1, out_width),
    )
    return (
        residual_out.reshape(steps, n, out_width),
        normed.reshape(steps, n, out_width),
        key_out[:, None],
        value_out[:, None],
    )


def solution(mesh):
    placed = (
        P(None, "group", "tensor", None),
        P(None, "group", "tensor", None),
        P(None, "group", "tensor", None),
        P("group", "tensor", None, None),
        P("group", "tensor", None, None),
        P(),
        P(),
        P(),
        P(None, "group", None),
        P("tensor", None),
        P(),
    )
    return jax.shard_map(
        on_device,
        mesh=mesh,
        in_specs=placed,
        out_specs=(
            P(None, "group", None),
            P(None, "group", None),
            P("group", "tensor", None, None),
            P("group", "tensor", None, None),
        ),
        check_vma=False,
    )
```
